128 devices in a mesh: patch: 32 (over z, y, core), dir: 4 (over x).
Axes of the slice: x: 4, y: 4, z: 4, core: 2. Of those that a mesh axis runs over, the one named last changes fastest.
Arguments:
- right_side: float32 [96, 768, 256], P('dir', 'patch'), may hold values from -6 to 6
- guess: float32 [96, 768, 256], P('dir', 'patch'), may hold values from -3 to 3
- mask_fine: int32 [96, 768, 2], P('dir', 'patch'), may hold values 0 or 1
- mask_next: int32 [48, 384, 1], P('dir', 'patch'), may hold values 0 or 1
Outputs:
- solution: float32 [96, 768, 256], P('dir', 'patch')
The draws below stay inside these ranges and needn't reach their ends.
All inputs are finite; a program needn't handle non-finite values. No bound on the sum of `mask_fine` or of `mask_next` on one device may be relied on, other than what follows from the above.
Results may differ from the reference program's by a relative error of at most 0.00005.
Values sent between devices are 32-bit elements; how exact they have to be, the bound alone decides.
No kernel may reach another device: no remote copies, remote signals or barrier semaphores. Data moves between devices by JAX's collectives and lax.ppermute only.
A program may use at most 64 MiB of HBM per device.

```python
import jax
import jax.numpy as jnp
from jax import lax

NW = 256
TILE = 128
SWEEPS = 3
LEVELS = 4
NU = 96
NV = 768


def with_ends(result, rng, low, top_value):
    index_at = [jax.random.randint(jax.random.fold_in(rng, axis), (), 0, length) for axis, length in enumerate(result.shape)]
    main_axis = result.shape.index(max(result.shape))
    neighbour = index_at[:main_axis] + [(index_at[main_axis] + 1) % result.shape[main_axis]] + index_at[main_axis + 1:]
    return result.at[tuple(index_at)].set(low).at[tuple(neighbour)].set(top_value)


def steps_of(rng, extent, cuts, smallest, largest):
    level, own = 1.0, jax.random.fold_in(rng, 6)
    for dim, blocks in cuts:
        steps = jnp.exp(jax.random.uniform(jax.random.fold_in(own, dim), (blocks,), jnp.float32, smallest / len(cuts), largest / len(cuts)))
        level = level * jnp.repeat(steps, extent[dim] // blocks).reshape([-1 if axis == dim else 1 for axis in range(len(extent))])
    return level


def normal_values(rng, dims, scale, most, shards=(), kind=jnp.bfloat16):
    values = jax.random.normal(rng, dims, jnp.float32) * scale
    if len(shards) > 0:
        values = steps_of(rng, dims, shards, -0.22, 0.18) * values
    return jnp.clip(values, min=-most, max=most).astype(kind)


def setup_inputs(seed: int = 0) -> dict:
    arg_keys = jax.random.split(jax.random.key(seed), 5)
    right_side = normal_values(arg_keys[0], (NU, NV, NW), 1.0, 6.0, ((0, 4), (1, 32)), jnp.float32)
    guess = normal_values(arg_keys[1], (NU, NV, NW), 0.5, 3.0, ((0, 4), (1, 32)), jnp.float32)
    mask_fine = with_ends((jax.random.randint(arg_keys[2], (NU, NV, NW // TILE), 0, 4) < 3).astype(jnp.int32), jax.random.fold_in(arg_keys[2], 1), 0, 1)
    mask_next = with_ends((jax.random.randint(arg_keys[3], (NU // 2, NV // 2, NW // (2 * TILE)), 0, 4) < 3).astype(jnp.int32), jax.random.fold_in(arg_keys[3], 1), 0, 1)
    return {"right_side": right_side, "guess": guess, "mask_fine": mask_fine, "mask_next": mask_next}


MASS = (1.0 / 5040, 120.0 / 5040, 1191.0 / 5040, 2416.0 / 5040, 1191.0 / 5040, 120.0 / 5040, 1.0 / 5040)
STIFF = (-1.0 / 120, -0.2, -0.125, 2.0 / 3, -0.125, -0.2, -1.0 / 120)
SUBDIV = (0.125, 0.5, 0.75, 0.5, 0.125)
OMEGA = 0.5


def wrap_pad(values, dimension, width, periodic):
    length = values.shape[dimension]
    if periodic:
        return jnp.concatenate([lax.slice_in_dim(values, length - width, length, axis=dimension), values, lax.slice_in_dim(values, 0, width, axis=dimension)], axis=dimension)
    widths = [(0, 0)] * values.ndim
    widths[dimension] = (width, width)
    return jnp.pad(values, widths)


def band_line(values, dimension, stencil, periodic):
    length = values.shape[dimension]
    padded = wrap_pad(values, dimension, 3, periodic)
    running = stencil[0] * lax.slice_in_dim(padded, 0, length, axis=dimension)
    for offset in range(1, 7):
        running = running + stencil[offset] * lax.slice_in_dim(padded, offset, offset + length, axis=dimension)
    return running


def restrict_line(values, dimension, periodic):
    halved = values.shape[dimension] // 2
    padded = wrap_pad(values, dimension, 2, periodic)
    running = SUBDIV[0] * lax.slice_in_dim(padded, 0, 2 * halved - 1, stride=2, axis=dimension)
    for offset in range(1, 5):
        running = running + SUBDIV[offset] * lax.slice_in_dim(padded, offset, offset + 2 * halved - 1, stride=2, axis=dimension)
    return running


def prolong_line(values, dimension, periodic):
    length = values.shape[dimension]
    padded = wrap_pad(values, dimension, 1, periodic)
    upper_part = lax.slice_in_dim(padded, 2, length + 2, axis=dimension)
    middle_part = lax.slice_in_dim(padded, 1, length + 1, axis=dimension)
    lower_part = lax.slice_in_dim(padded, 0, length, axis=dimension)
    even_part = SUBDIV[0] * upper_part + SUBDIV[2] * middle_part + SUBDIV[4] * lower_part
    odd_part = SUBDIV[1] * upper_part + SUBDIV[3] * middle_part
    joined = jnp.stack([even_part, odd_part], axis=dimension + 1)
    old_shape = values.shape
    return joined.reshape(old_shape[:dimension] + (2 * length,) + old_shape[dimension + 1:])


def operate(current, scale_factor):
    mass_side = band_line(current, 2, MASS, False)
    stiff_side = band_line(current, 2, STIFF, False)
    first_term = band_line(mass_side, 1, MASS, True)
    second = band_line(mass_side, 1, STIFF, True) + band_line(stiff_side, 1, MASS, True)
    return scale_factor * (band_line(first_term, 0, STIFF, False) + band_line(second, 0, MASS, False))


def smooth(current, load, scale_factor, active):
    update = (OMEGA / scale_factor) * (load - operate(current, scale_factor))
    if active is not None:
        update = update * active
    return current + update


def cycle(load, current, level_index, actives):
    scale_factor = float(2 ** level_index)
    active = actives[level_index]
    for sweep_index in range(SWEEPS):
        current = smooth(current, load, scale_factor, active)
    if level_index + 1 < LEVELS:
        residual_field = load - operate(current, scale_factor)
        if active is not None:
            residual_field = residual_field * active
        coarse_load = restrict_line(restrict_line(restrict_line(residual_field, 2, False), 1, True), 0, False)
        correction = cycle(coarse_load, jnp.zeros_like(coarse_load), level_index + 1, actives)
        finer = prolong_line(prolong_line(prolong_line(correction, 2, False), 1, True), 0, False)
        if active is not None:
            finer = finer * active
        current = current + finer
    for sweep_index in range(SWEEPS):
        current = smooth(current, load, scale_factor, active)
    return current


def reference(right_side, guess, mask_fine, mask_next):
    actives = [jnp.repeat(mask_fine.astype(jnp.float32), TILE, axis=2), jnp.repeat(mask_next.astype(jnp.float32), TILE, axis=2)] + [None] * (LEVELS - 2)
    return cycle(right_side, guess * actives[0], 0, actives)
```

```python
import functools

import jax
import jax.numpy as jnp
from jax import lax
from jax.experimental import pallas as pl
from jax.experimental.pallas import tpu as pltpu
from jax.sharding import Mesh
from jax.sharding import PartitionSpec as P

F32 = jnp.float32
BF16 = jnp.bfloat16
LANES = 128

MASS = (2416.0, 1191.0, 120.0, 1.0)
STIFF = (80.0, -15.0, -24.0, -1.0)
ALPHA = 0.5 / (120.0 * 5040.0 * 5040.0)
PATCH = ("pz", "core")


def dot(a, b):
    return jnp.dot(a, b, preferred_element_type=F32)


def split(value):
    high = value.astype(BF16)
    return high, (value - high.astype(F32)).astype(BF16)


def dot_split(value, matrix):
    high, low = split(value)
    return dot(high, matrix) + dot(low, matrix)


def banded(rows, columns, size_r, size_c, coeffs, row_step, column_step):
    i = lax.broadcasted_iota(jnp.int32, (rows, columns), 0)
    j = lax.broadcasted_iota(jnp.int32, (rows, columns), 1)
    at = row_step * i + column_step * j
    out = jnp.zeros((rows, columns), F32)
    for key, weight in coeffs.items():
        out = jnp.where(at == key, weight, out)
    return jnp.where((i < size_r) & (j < size_c), out, 0.0).astype(BF16)


def fill_w(w_ref, depth, size):
    mass = {0: 2416.0, 1: 1192.0, -1: 1192.0, 2: 120.0, -2: 120.0, 3: 1.0, -3: 1.0}
    low = {1: -1.0, -1: -1.0}
    stiff = {0: 80.0, 1: -15.0, -1: -15.0, 2: -24.0, -2: -24.0, 3: -1.0, -3: -1.0}
    for block, table in enumerate((mass, mass, stiff, stiff, low)):
        w_ref[block * depth : (block + 1) * depth, :] = banded(
            depth, depth, size, size, table, 1, -1
        )


def restrict_w(rows, columns, size):
    taps = {-2: 0.125, -1: 0.5, 0: 0.75, 1: 0.5, 2: 0.125}
    return banded(rows, columns, size, size // 2, taps, 1, -2)


def prolong_w(rows, columns, size):
    taps = {-2: 0.125, -1: 0.5, 0: 0.75, 1: 0.5, 2: 0.125}
    return banded(rows, columns, size // 2, size, taps, -2, 1)


def stencil(x_ref, l_ref, u0, nu, v0, nv):
    tiles = x_ref.shape[0]
    depth = tiles * LANES

    def weigh(centre, one, two, three, taps):
        return taps[0] * centre + taps[1] * one + taps[2] * two + taps[3] * three

    for tile in range(tiles):
        for column in range(nv // 16):
            row = v0 + 16 * column

            def plane(u):
                x = [x_ref[tile, u, pl.ds(row - 3 + k, 16), :] for k in range(7)]
                one, two, three = x[2] + x[4], x[1] + x[5], x[0] + x[6]
                p = 2416.0 * x[3] + 1191.0 * one + 120.0 * two + three
                q = 80.0 * x[3] - 15.0 * one - 24.0 * two - three
                return p, q

            def emit(at, ps, qs):
                p1, p2, p3 = ps[2] + ps[4], ps[1] + ps[5], ps[0] + ps[6]
                q1, q2, q3 = qs[2] + qs[4], qs[1] + qs[5], qs[0] + qs[6]
                r = 2416.0 * ps[3] + 1191.0 * p1 + 120.0 * p2 + p3
                s = (80.0 * ps[3] - 15.0 * p1 - 24.0 * p2 - p3) + (
                    2416.0 * qs[3] + 1191.0 * q1 + 120.0 * q2 + q3
                )
                for part, value in enumerate(split(s) + split(r)):
                    lane = part * depth + tile * LANES
                    l_ref[at, 16 * column : 16 * column + 16, lane : lane + LANES] = value

            def several(first, count, carry):
                ps, qs = list(carry[:6]), list(carry[6:])
                for k in range(count):
                    p, q = plane(u0 + first + k + 3)
                    emit(first + k, ps + [p], qs + [q])
                    ps, qs = ps[1:] + [p], qs[1:] + [q]
                return tuple(ps + qs)

            start = [plane(u0 - 3 + k) for k in range(6)]
            carry = tuple([p for p, _ in start] + [q for _, q in start])
            groups = nu // 6
            if groups > 1:
                carry = lax.fori_loop(0, groups, lambda g, c: several(6 * g, 6, c), carry)
            elif groups == 1:
                carry = several(0, 6, carry)
            if nu % 6:
                several(6 * groups, nu % 6, carry)


def finish(l_ref, w_ref, nu, nv, use):
    depth = w_ref.shape[1]
    chunk = max(1, min(nu, 384 // nv))

    def some(first, count):
        left = l_ref[pl.ds(first, count), 0:nv, :].reshape(count * nv, 4 * depth)
        use(
            first,
            count,
            dot(left, w_ref[0 : 4 * depth, :])
            + dot(left[:, 0:depth], w_ref[4 * depth : 5 * depth, :]),
        )

    whole = nu // chunk
    if whole > 1:
        lax.fori_loop(0, whole, lambda c, _: some(c * chunk, chunk), None)
    elif whole == 1:
        some(0, chunk)
    if nu % chunk:
        some(whole * chunk, nu % chunk)


def sweep(x_ref, sf_ref, sa, l_ref, w_ref, u0, nu, v0, nv):
    stencil(x_ref, l_ref, u0, nu, v0, nv)

    def use(first, count, product):
        for tile in range(x_ref.shape[0]):
            at = (tile, pl.ds(u0 + first, count), pl.ds(v0, nv), slice(None))
            part = product[:, tile * LANES : (tile + 1) * LANES].reshape(count, nv, LANES)
            weight = sa if isinstance(sa, float) else sa[at]
            x_ref[at] = x_ref[at] + (sf_ref[at] - weight * part)

    finish(l_ref, w_ref, nu, nv, use)


def residual(x_ref, sf_ref, sa, l_ref, w_ref, rw, t_ref, scale, u0, nu, v0, nv, t0):
    stencil(x_ref, l_ref, u0, nu, v0, nv)

    def use(first, count, product):
        parts = []
        for tile in range(x_ref.shape[0]):
            at = (tile, pl.ds(u0 + first, count), pl.ds(v0, nv), slice(None))
            part = product[:, tile * LANES : (tile + 1) * LANES].reshape(count, nv, LANES)
            weight = sa if isinstance(sa, float) else sa[at]
            value = scale * (sf_ref[at] - weight * part)
            parts.append(value.reshape(count * nv, LANES))
        whole = parts[0] if len(parts) == 1 else jnp.concatenate(parts, axis=1)
        narrow = dot_split(whole, rw)
        t_ref[pl.ds(t0 + first, count), 0:nv, :] = narrow.reshape(count, nv, LANES)

    finish(l_ref, w_ref, nu, nv, use)


def narrow_plane(t_ref, tu_ref, j, nv, rows):
    at = [t_ref[2 * j + k, 0:nv, :] for k in range(5)]
    tu_ref[0:nv, :] = 0.125 * (at[0] + at[4]) + 0.5 * (at[1] + at[3]) + 0.75 * at[2]
    at = [tu_ref[pl.ds(k, rows, stride=2), :] for k in range(5)]
    return 0.125 * (at[0] + at[4]) + 0.5 * (at[1] + at[3]) + 0.75 * at[2]


def widen(read, even, tu_ref, z_ref, slot, rows):
    if even:
        plane = 0.125 * (read(-1) + read(1)) + 0.75 * read(0)
    else:
        plane = 0.5 * (read(0) + read(1))
    tu_ref[0 : plane.shape[0], :] = plane
    low, mid, high = (tu_ref[k : k + rows, :] for k in range(3))
    z_ref[slot, pl.ds(0, rows, stride=2), :] = 0.125 * (low + high) + 0.75 * mid
    z_ref[slot, pl.ds(1, rows, stride=2), :] = 0.5 * (mid + high)


def spread_mask(column, rows):
    return jnp.broadcast_to(column, (rows, LANES))


UB0, VB0, V0 = 14, 16, 64


def fill_fine(own, low, high, mask, x_ref, sf_ref, sa_ref):
    parts = ((low, 0, 16), (own, 16, 24), (high, 40, 16))
    for u in range(51):
        for tile in range(2):
            for source, row, rows in parts:
                at = slice(row, row + rows)
                lanes = slice(tile * LANES, (tile + 1) * LANES)
                lane = 2 * u + tile
                active = spread_mask(mask[at, lane : lane + 1], rows)
                if x_ref is not None:
                    x_ref[tile, u, at, :] = active * source[u, :, lanes]
                if 3 <= u < 48:
                    sa_ref[tile, u, at, :] = ALPHA * active
                    sf_ref[tile, u, at, :] = (0.5 * active) * source[51 + u - 3, :, lanes]


def fine_pre(own, low, high, mask, x_out, f1_out, x, sf, sa, l_ref, w_ref, t_ref, tu_ref):
    fill_w(w_ref, 256, 256)
    fill_fine(own, low, high, mask, x, sf, sa)
    sweep(x, sf, sa, l_ref, w_ref, 3, 45, 5, 48)
    sweep(x, sf, sa, l_ref, w_ref, 6, 39, 8, 48)
    sweep(x, sf, sa, l_ref, w_ref, 9, 33, 11, 48)
    for tile in range(2):
        x_out[:, :, tile * LANES : (tile + 1) * LANES] = x[tile, 14:38, 16:40, :]
    rw = restrict_w(256, LANES, 256)
    residual(x, sf, sa, l_ref, w_ref, rw, t_ref, 2.0, 12, 27, 14, 32, 0)
    for j in range(12):
        f1_out[j] = narrow_plane(t_ref, tu_ref, j, 32, 12)


def fine_post(
    own, low, high, mask, x_own, x_low, x_high, e_own, e_low, e_high,
    out, x, sf, sa, l_ref, w_ref, e_ref, tu_ref, z_ref,
):
    fill_w(w_ref, 256, 256)
    fill_fine(own, low, high, mask, None, sf, sa)
    e_ref[:, 0:8, :] = e_low[...]
    e_ref[:, 8:20, :] = e_own[...]
    e_ref[:, 20:28, :] = e_high[...]
    pw = prolong_w(LANES, 256, 256)
    position = lax.axis_index("dir")

    def one(i, even):
        u = 2 * i - 10 + (0 if even else 1)
        coarse = i + 1

        def read(k):
            at = coarse + k
            place = 12 * position + at - 6
            inside = jnp.logical_and(place >= 0, place < 48)
            return jnp.where(inside, e_ref[at, 2:26, :], 0.0)

        widen(read, even, tu_ref, z_ref, 0, 22)
        fine = dot_split(z_ref[0, 0:48, :], pw)
        at = u + UB0
        for tile in range(2):
            lanes = slice(tile * LANES, (tile + 1) * LANES)
            x[tile, at, 6:50, :] = fine[0:44, lanes]

    for i in range(22):
        for even in (True, False):
            u = 2 * i - 10 + (0 if even else 1)
            if -9 <= u <= 32:
                one(i, even)
    for u in range(42):
        for tile in range(2):
            lanes = slice(tile * LANES, (tile + 1) * LANES)
            at = u + 5
            for source, row, rows in ((x_low, 0, 16), (x_own, 16, 24), (x_high, 40, 16)):
                part = slice(row, row + rows)
                active = spread_mask(mask[part, 2 * at + tile : 2 * at + tile + 1], rows)
                x[tile, at, part, :] = active * (x[tile, at, part, :] + source[u, :, lanes])
    sweep(x, sf, sa, l_ref, w_ref, 8, 36, 10, 48)
    sweep(x, sf, sa, l_ref, w_ref, 11, 30, 13, 32)
    sweep(x, sf, sa, l_ref, w_ref, 14, 24, 16, 32)
    for tile in range(2):
        out[:, :, tile * LANES : (tile + 1) * LANES] = x[tile, 14:38, 16:40, :]


def fill_next(own, low, high, mask, x_ref, sf_ref, sa_ref):
    for u in range(36):
        for source, row in ((low, 0), (own, 12), (high, 24)):
            at = slice(row, row + 12)
            active = spread_mask(mask[at, u : u + 1], 12)
            value = (0.25 * active) * source[u]
            sa_ref[0, u, at, :] = ALPHA * active
            sf_ref[0, u, at, :] = value
            if x_ref is not None:
                x_ref[0, u, at, :] = value


def next_pre(own, low, high, mask, x_out, f2_out, x, sf, sa, l_ref, w_ref, t_ref, tu_ref):
    fill_w(w_ref, 128, 128)
    fill_next(own, low, high, mask, x, sf, sa)
    sweep(x, sf, sa, l_ref, w_ref, 4, 27, 4, 32)
    sweep(x, sf, sa, l_ref, w_ref, 7, 21, 7, 32)
    x_out[...] = x[0, 12:24, 12:24, :]
    rw = restrict_w(LANES, LANES, 128)
    residual(x, sf, sa, l_ref, w_ref, rw, t_ref, 4.0, 10, 15, 10, 16, 0)
    for j in range(3):
        even = narrow_plane(t_ref, tu_ref, 2 * j, 16, 6)
        odd = narrow_plane(t_ref, tu_ref, 2 * j + 1, 16, 6)
        f2_out[6 * j : 6 * j + 6, :] = even + pltpu.roll(odd, 64, 1)


def next_post(
    own, low, high, mask, x_own, x_low, x_high, e2,
    out, x, sf, sa, l_ref, w_ref, tu_ref, z_ref,
):
    fill_w(w_ref, 128, 128)
    fill_next(own, low, high, mask, None, sf, sa)
    for u in range(36):
        for source, row in ((x_low, 0), (x_own, 12), (x_high, 24)):
            x[0, u, row : row + 12, :] = source[u]
    pw = prolong_w(LANES, LANES, 128)
    for u in range(-9, 21):
        coarse = u // 2 + 5

        def read(k):
            return e2[coarse + k, 0:24, :]

        widen(read, u % 2 == 0, tu_ref, z_ref, 0, 16)
        first = 0.5 * (tu_ref[0:1, :] + tu_ref[1:2, :])
        fine = dot_split(z_ref[0, 0:32, :], pw)
        ahead = dot_split(jnp.broadcast_to(first, (16, LANES)), pw)
        x[0, u + 12, 4:36, :] = x[0, u + 12, 4:36, :] + fine
        x[0, u + 12, 3:4, :] = x[0, u + 12, 3:4, :] + ahead[0:1]
    for u in range(3, 33):
        for row in range(0, 36, 12):
            at = slice(row, row + 12)
            active = spread_mask(mask[at, u : u + 1], 12)
            x[0, u, at, :] = active * x[0, u, at, :]
    sweep(x, sf, sa, l_ref, w_ref, 6, 24, 6, 32)
    sweep(x, sf, sa, l_ref, w_ref, 9, 18, 9, 32)
    sweep(x, sf, sa, l_ref, w_ref, 12, 12, 12, 16)
    out[...] = x[0, 12:24, 12:24, :]


def coarse(same, other, e_out, x, sf, l_ref, w_ref, t_ref, tu_ref, x3, sf3, w3_ref, z_ref):
    fill_w(w_ref, 128, 64)
    fill_w(w3_ref, 128, 32)
    pair, core = lax.axis_index("pz"), lax.axis_index("core")
    position = lax.axis_index("dir")
    lane = lax.broadcasted_iota(jnp.int32, (6, LANES), 1)
    low_half = lane < 64

    for edge in (0, 1, 2, 27, 28, 29):
        x[0, edge] = jnp.zeros(x.shape[2:], F32)
    for edge in (0, 1, 26, 27, 28):
        t_ref[edge] = jnp.zeros(t_ref.shape[1:], F32)

    def place(source, offset, row):
        index = lax.rem(pair + 16 + offset, 16)
        for d in range(4):
            for k in range(3):
                both = 0.125 * source[index * 4 + d, 6 * k : 6 * k + 6, :]
                for odd in (0, 1):
                    value = pltpu.roll(both, 64, 1) if odd else both
                    value = jnp.where(low_half, value, 0.0)
                    u = 6 * d + 2 * k + odd + 3
                    x[0, u, pl.ds(row, 6), :] = value
                    sf[0, u, pl.ds(row, 6), :] = value

    def even_patch(k, _):
        place(same, k - 5, 12 * k)

    def odd_patch(k, _):
        place(other, k - 5 + core, 12 * k + 6)

    lax.fori_loop(0, 11, even_patch, None)
    lax.fori_loop(0, 10, odd_patch, None)

    sweep(x, sf, ALPHA, l_ref, w_ref, 3, 24, 6, 128)
    sweep(x, sf, ALPHA, l_ref, w_ref, 3, 24, 9, 112)
    rw = restrict_w(LANES, LANES, 64)
    residual(x, sf, ALPHA, l_ref, w_ref, rw, t_ref, 8.0, 3, 24, 12, 112, 2)

    for edge in (0, 1, 2, 15, 16, 17):
        x3[0, edge] = jnp.zeros(x3.shape[2:], F32)

    def narrow(j, _):
        value = 0.0625 * narrow_plane(t_ref, tu_ref, j, 112, 50)
        x3[0, j + 3, 3:53, :] = value
        sf3[0, j + 3, 3:53, :] = value

    lax.fori_loop(0, 12, narrow, None)
    sweep(x3, sf3, ALPHA, l_ref, w3_ref, 3, 12, 6, 48)
    sweep(x3, sf3, ALPHA, l_ref, w3_ref, 3, 12, 9, 48)
    sweep(x3, sf3, ALPHA, l_ref, w3_ref, 3, 12, 12, 32)
    sweep(x3, sf3, ALPHA, l_ref, w3_ref, 3, 12, 15, 32)
    sweep(x3, sf3, ALPHA, l_ref, w3_ref, 3, 12, 18, 32)

    pw = prolong_w(LANES, LANES, 64)

    def wide(j, _):
        def read(k):
            return x3[0, j + 3 + k, 18:42, :]

        for odd in (0, 1):
            widen(read, not odd, tu_ref, z_ref, odd, 22)
            fine = dot_split(z_ref[odd, 0:48, :], pw)
            at = (0, 2 * j + odd + 3, slice(46, 94), slice(None))
            x[at] = x[at] + fine

    lax.fori_loop(0, 12, wide, None)
    sweep(x, sf, ALPHA, l_ref, w_ref, 3, 24, 49, 32)
    sweep(x, sf, ALPHA, l_ref, w_ref, 3, 24, 52, 32)
    sweep(x, sf, ALPHA, l_ref, w_ref, 3, 24, 55, 32)

    def give(k, _):
        u = 6 * position - 5 + k
        inside = jnp.logical_and(u >= 0, u < 24)
        at = jnp.clip(u, 0, 23) + 3
        e_out[k] = jnp.where(inside, x[0, at, 55:79, :], 0.0)

    lax.fori_loop(0, 17, give, None)


def call(body, outs, scratch, operands, flops):
    vmem = pl.BlockSpec(memory_space=pltpu.VMEM)
    size = 0
    for array in list(operands) + list(outs):
        dims = list(array.shape)
        dims[-1] = -(-dims[-1] // 128) * 128
        dims[-2] = -(-dims[-2] // 16) * 16
        count = 1
        for dim in dims:
            count *= dim
        size += 4 * count
    for shape, kind in scratch:
        count = 1
        for dim in shape:
            count *= dim
        size += count * (2 if kind == BF16 else 4)
    return pl.pallas_call(
        body,
        out_shape=list(outs),
        in_specs=[vmem] * len(operands),
        out_specs=[vmem] * len(outs),
        scratch_shapes=[pltpu.VMEM(shape, kind) for shape, kind in scratch],
        compiler_params=pltpu.CompilerParams(vmem_limit_bytes=size + (6 << 20)),
        cost_estimate=pl.CostEstimate(flops=flops, bytes_accessed=size, transcendentals=0),
    )(*operands)


def shape_of(*dims):
    return jax.ShapeDtypeStruct(dims, F32)


def ring(value, axes, step):
    count = 1
    for axis in axes:
        count *= lax.axis_size(axis)
    pairs = [(i, (i + step) % count) for i in range(count)]
    return lax.ppermute(value, axes if len(axes) > 1 else axes[0], pairs)


def along_dir(value, before, after):
    count = value.shape[0]
    low = ring(value[count - before :], ("dir",), 1)
    high = ring(value[:after], ("dir",), -1)
    return low, high


def around_next(value):
    low, high = along_dir(value, 12, 12)
    extended = jnp.concatenate([low, value, high], axis=0)
    return extended, ring(extended, PATCH, 1), ring(extended, PATCH, -1)


def inside_lanes(first, count, per, total):
    plane = first + jnp.arange(count) // per
    return ((plane >= 0) & (plane < total)).astype(F32)


def on_device(right_side, guess, mask_fine, mask_next):
    position = lax.axis_index("dir")
    fine = jnp.transpose(mask_fine, (1, 0, 2)).reshape(24, 48).astype(F32)
    following = mask_next[:, :, 0].T.astype(F32)
    plane = jnp.concatenate(
        [
            jnp.pad(fine, ((0, 0), (0, 80))),
            jnp.pad(following, ((0, 12), (0, 116))),
        ],
        axis=1,
    )[None]
    up = jnp.concatenate([guess[10:], right_side[13:], plane], axis=0)
    down = jnp.concatenate([guess[:13], right_side[:10], plane], axis=0)
    low = ring(up, ("dir",), 1)
    high = ring(down, ("dir",), -1)
    m_low, m_high, m_own = low[25], high[23], plane[0]
    fine = jnp.concatenate([m_low[:, 20:48], m_own[:, :48], m_high[:, :26]], axis=1)
    fine = fine * inside_lanes(24 * position - 14, 102, 2, 96)
    following = jnp.concatenate(
        [m_low[:12, 128:140], m_own[:12, 128:140], m_high[:12, 128:140]], axis=1
    )
    following = following * inside_lanes(12 * position - 12, 36, 1, 48)
    plane = jnp.concatenate(
        [
            jnp.pad(fine, ((0, 0), (0, 26))),
            jnp.pad(following, ((12, 0), (0, 28))) + jnp.zeros((24, 64), F32),
            jnp.pad(following, ((0, 12), (0, 28))) + jnp.zeros((24, 64), F32),
        ],
        axis=1,
    )[None]
    own = jnp.concatenate(
        [low[:14], guess, high[:13], low[14:25], right_side, high[13:23], plane], axis=0
    )
    low = ring(own[:, 8:24], PATCH, 1)
    high = ring(own[:, 0:16], PATCH, -1)
    mask0 = jnp.concatenate([low[96, :, :128], own[96, :, :128], high[96, :, :128]], axis=0)
    mask1 = jnp.concatenate(
        [low[96, 4:16, 128:192], own[96, 12:24, 128:192], high[96, 0:12, 192:256]], axis=0
    )
    mask1 = jnp.pad(mask1, ((0, 4), (0, 64)))

    window = ((2, 52, V0, LANES), F32)
    left0 = ((46, 48, 1024), BF16)
    w0 = ((1280, 256), BF16)
    x0, f1 = call(
        fine_pre,
        [shape_of(24, 24, 256), shape_of(12, 12, 128)],
        [window, window, window, left0, w0, ((28, 32, 128), F32), ((48, 128), F32)],
        (own, low, high, mask0),
        10**10,
    )

    f1_own, f1_low, f1_high = around_next(f1)
    window1 = ((1, 36, 48, LANES), F32)
    left1 = ((28, 32, 512), BF16)
    w1 = ((640, 128), BF16)
    x1, f2 = call(
        next_pre,
        [shape_of(12, 12, 128), shape_of(18, 128)],
        [window1, window1, window1, left1, w1, ((16, 16, 128), F32), ((48, 128), F32)],
        (f1_own, f1_low, f1_high, mask1),
        10**9,
    )

    x0_low, x0_high = along_dir(x0, 9, 9)
    x0_own = jnp.concatenate([x0_low, x0, x0_high], axis=0)
    x0_low = ring(x0_own[:, 8:24], PATCH, 1)
    x0_high = ring(x0_own[:, 0:16], PATCH, -1)
    x1_own, x1_low, x1_high = around_next(x1)

    same = lax.all_to_all(jnp.broadcast_to(f2[None], (64, 18, 128)), ("pz", "dir"), 0, 0)
    other = lax.ppermute(same, "core", [(0, 1), (1, 0)])
    (e2,) = call(
        coarse,
        [shape_of(17, 24, 128)],
        [
            ((1, 30, 144, LANES), F32),
            ((1, 30, 144, LANES), F32),
            ((24, 128, 512), BF16),
            w1,
            ((29, 112, 128), F32),
            ((112, 128), F32),
            ((1, 18, 64, LANES), F32),
            ((1, 18, 64, LANES), F32),
            w1,
            ((2, 48, 128), F32),
        ],
        (same, other),
        4 * 10**9,
    )
    (e1,) = call(
        next_post,
        [shape_of(12, 12, 128)],
        [window1, window1, window1, left1, w1, ((48, 128), F32), ((2, 48, 128), F32)],
        (f1_own, f1_low, f1_high, mask1, x1_own, x1_low, x1_high, e2),
        10**9,
    )
    e1_low, e1_high = along_dir(e1, 6, 6)
    e1_own = jnp.concatenate([e1_low, e1, e1_high], axis=0)
    e1_low = ring(e1_own[:, 4:12], PATCH, 1)
    e1_high = ring(e1_own[:, 0:8], PATCH, -1)
    (out,) = call(
        fine_post,
        [shape_of(24, 24, 256)],
        [
            window,
            window,
            window,
            left0,
            w0,
            ((24, 32, 128), F32),
            ((48, 128), F32),
            ((2, 48, 128), F32),
        ],
        (own, low, high, mask0, x0_own, x0_low, x0_high, e1_own, e1_low, e1_high),
        10**10,
    )
    return out


def solution(mesh):
    pairs = Mesh(mesh.devices.reshape(16, 2, 4), ("pz", "core", "dir"))
    spec = P("dir", PATCH, None)
    return jax.shard_map(
        on_device, mesh=pairs, in_specs=(spec,) * 4, out_specs=spec, check_vma=False
    )
```

```python
import functools

import jax
import jax.numpy as jnp
from jax import lax
from jax.experimental import pallas as pl
from jax.experimental.pallas import tpu as pltpu
from jax.sharding import Mesh
from jax.sharding import PartitionSpec as P

F32 = jnp.float32
BF16 = jnp.bfloat16
LANES = 128

MASS = (2416.0, 1191.0, 120.0, 1.0)
STIFF = (80.0, -15.0, -24.0, -1.0)
ALPHA = 0.5 / (120.0 * 5040.0 * 5040.0)
PATCH = ("pz", "core")


def dot(a, b):
    return jnp.dot(a, b, preferred_element_type=F32)


def split(value):
    high = value.astype(BF16)
    return high, (value - high.astype(F32)).astype(BF16)


def dot_split(value, matrix):
    high, low = split(value)
    return dot(high, matrix) + dot(low, matrix)


def banded(rows, columns, size_r, size_c, coeffs, row_step, column_step, pairs=False):
    i = lax.broadcasted_iota(jnp.int32, (rows, columns), 0)
    j = lax.broadcasted_iota(jnp.int32, (rows, columns), 1)
    same = i >= 0
    if pairs:
        same = (i < 64) == (j < 64)
        i, j = jnp.where(i < 64, i, i - 64), jnp.where(j < 64, j, j - 64)
    at = row_step * i + column_step * j
    out = jnp.zeros((rows, columns), F32)
    for key, weight in coeffs.items():
        out = jnp.where(at == key, weight, out)
    return jnp.where((i < size_r) & (j < size_c) & same, out, 0.0).astype(BF16)


def fill_w(w_ref, depth, size, pairs=False):
    mass = {0: 2416.0, 1: 1192.0, -1: 1192.0, 2: 120.0, -2: 120.0, 3: 1.0, -3: 1.0}
    low = {1: -1.0, -1: -1.0}
    stiff = {0: 80.0, 1: -15.0, -1: -15.0, 2: -24.0, -2: -24.0, 3: -1.0, -3: -1.0}
    for block, table in enumerate((mass, mass, stiff, stiff, low)):
        w_ref[block * depth : (block + 1) * depth, :] = banded(
            depth, depth, size, size, table, 1, -1, pairs
        )


def restrict_w(rows, columns, size, pairs=False):
    taps = {-2: 0.125, -1: 0.5, 0: 0.75, 1: 0.5, 2: 0.125}
    return banded(rows, columns, size, size // 2, taps, 1, -2, pairs)


def prolong_w(rows, columns, size, pairs=False):
    taps = {-2: 0.125, -1: 0.5, 0: 0.75, 1: 0.5, 2: 0.125}
    return banded(rows, columns, size // 2, size, taps, -2, 1, pairs)


def stencil(x_ref, l_ref, u0, nu, v0, nv):
    tiles = x_ref.shape[0]
    depth = tiles * LANES

    def weigh(centre, one, two, three, taps):
        return taps[0] * centre + taps[1] * one + taps[2] * two + taps[3] * three

    for tile in range(tiles):
        for column in range(nv // 16):
            row = v0 + 16 * column

            def plane(u):
                x = [x_ref[tile, u, pl.ds(row - 3 + k, 16), :] for k in range(7)]
                one, two, three = x[2] + x[4], x[1] + x[5], x[0] + x[6]
                p = 2416.0 * x[3] + 1191.0 * one + 120.0 * two + three
                q = 80.0 * x[3] - 15.0 * one - 24.0 * two - three
                return p, q

            def emit(at, ps, qs):
                p1, p2, p3 = ps[2] + ps[4], ps[1] + ps[5], ps[0] + ps[6]
                q1, q2, q3 = qs[2] + qs[4], qs[1] + qs[5], qs[0] + qs[6]
                r = 2416.0 * ps[3] + 1191.0 * p1 + 120.0 * p2 + p3
                s = (80.0 * ps[3] - 15.0 * p1 - 24.0 * p2 - p3) + (
                    2416.0 * qs[3] + 1191.0 * q1 + 120.0 * q2 + q3
                )
                for part, value in enumerate(split(s) + split(r)):
                    lane = part * depth + tile * LANES
                    l_ref[at, 16 * column : 16 * column + 16, lane : lane + LANES] = value

            def several(first, count, carry):
                ps, qs = list(carry[:6]), list(carry[6:])
                for k in range(count):
                    p, q = plane(u0 + first + k + 3)
                    emit(first + k, ps + [p], qs + [q])
                    ps, qs = ps[1:] + [p], qs[1:] + [q]
                return tuple(ps + qs)

            start = [plane(u0 - 3 + k) for k in range(6)]
            carry = tuple([p for p, _ in start] + [q for _, q in start])
            groups = nu // 6
            if groups > 1:
                carry = lax.fori_loop(0, groups, lambda g, c: several(6 * g, 6, c), carry)
            elif groups == 1:
                carry = several(0, 6, carry)
            if nu % 6:
                several(6 * groups, nu % 6, carry)


def stencil_pairs(x_ref, l_ref, k0, nk, v0, nv):
    low = lax.broadcasted_iota(jnp.int32, (16, LANES), 1) < 64

    for column in range(nv // 16):
        row = v0 + 16 * column

        def plane(k):
            x = [x_ref[0, k, pl.ds(row - 3 + i, 16), :] for i in range(7)]
            one, two, three = x[2] + x[4], x[1] + x[5], x[0] + x[6]
            p = 2416.0 * x[3] + 1191.0 * one + 120.0 * two + three
            q = 80.0 * x[3] - 15.0 * one - 24.0 * two - three
            return p, pltpu.roll(p, 64, 1), q, pltpu.roll(q, 64, 1)

        def sums(own, other):
            one = other[2] + jnp.where(low, other[1], other[3])
            three = jnp.where(low, other[0], other[4]) + jnp.where(low, other[3], other[1])
            return own[2], one, own[1] + own[3], three

        def emit(at, planes):
            p, p1, p2, p3 = sums([t[0] for t in planes], [t[1] for t in planes])
            q, q1, q2, q3 = sums([t[2] for t in planes], [t[3] for t in planes])
            r = 2416.0 * p + 1191.0 * p1 + 120.0 * p2 + p3
            s = (80.0 * p - 15.0 * p1 - 24.0 * p2 - p3) + (
                2416.0 * q + 1191.0 * q1 + 120.0 * q2 + q3
            )
            for part, value in enumerate(split(s) + split(r)):
                l_ref[at, 16 * column : 16 * column + 16, part * LANES : (part + 1) * LANES] = value

        def several(first, count, carry):
            planes = [carry[4 * i : 4 * i + 4] for i in range(4)]
            for i in range(count):
                planes = planes + [plane(k0 + first + i + 2)]
                emit(first + i, planes)
                planes = planes[1:]
            return tuple(value for t in planes for value in t)

        carry = tuple(value for i in range(4) for value in plane(k0 - 2 + i))
        if nk > 6:
            lax.fori_loop(0, nk // 4, lambda g, c: several(4 * g, 4, c), carry)
        else:
            several(0, nk, carry)


def finish(l_ref, w_ref, nu, nv, use):
    depth = w_ref.shape[1]
    chunk = max(1, min(nu, 384 // nv))

    def some(first, count):
        left = l_ref[pl.ds(first, count), 0:nv, :].reshape(count * nv, 4 * depth)
        use(
            first,
            count,
            dot(left, w_ref[0 : 4 * depth, :])
            + dot(left[:, 0:depth], w_ref[4 * depth : 5 * depth, :]),
        )

    whole = nu // chunk
    if whole > 1:
        lax.fori_loop(0, whole, lambda c, _: some(c * chunk, chunk), None)
    elif whole == 1:
        some(0, chunk)
    if nu % chunk:
        some(whole * chunk, nu % chunk)


def sweep(x_ref, sf_ref, sa, l_ref, w_ref, u0, nu, v0, nv, apply=stencil):
    apply(x_ref, l_ref, u0, nu, v0, nv)

    def use(first, count, product):
        for tile in range(x_ref.shape[0]):
            at = (tile, pl.ds(u0 + first, count), pl.ds(v0, nv), slice(None))
            part = product[:, tile * LANES : (tile + 1) * LANES].reshape(count, nv, LANES)
            weight = sa if isinstance(sa, float) else sa[at]
            x_ref[at] = x_ref[at] + (sf_ref[at] - weight * part)

    finish(l_ref, w_ref, nu, nv, use)


def residual(x_ref, sf_ref, sa, l_ref, w_ref, rw, t_ref, scale, u0, nu, v0, nv, t0, apply=stencil):
    apply(x_ref, l_ref, u0, nu, v0, nv)

    def use(first, count, product):
        parts = []
        for tile in range(x_ref.shape[0]):
            at = (tile, pl.ds(u0 + first, count), pl.ds(v0, nv), slice(None))
            part = product[:, tile * LANES : (tile + 1) * LANES].reshape(count, nv, LANES)
            weight = sa if isinstance(sa, float) else sa[at]
            value = scale * (sf_ref[at] - weight * part)
            parts.append(value.reshape(count * nv, LANES))
        whole = parts[0] if len(parts) == 1 else jnp.concatenate(parts, axis=1)
        narrow = dot_split(whole, rw)
        t_ref[pl.ds(t0 + first, count), 0:nv, :] = narrow.reshape(count, nv, LANES)

    finish(l_ref, w_ref, nu, nv, use)


def narrow_plane(t_ref, tu_ref, j, nv, rows):
    at = [t_ref[2 * j + k, 0:nv, :] for k in range(5)]
    tu_ref[0:nv, :] = 0.125 * (at[0] + at[4]) + 0.5 * (at[1] + at[3]) + 0.75 * at[2]
    at = [tu_ref[pl.ds(k, rows, stride=2), :] for k in range(5)]
    return 0.125 * (at[0] + at[4]) + 0.5 * (at[1] + at[3]) + 0.75 * at[2]


def widen(read, even, tu_ref, z_ref, slot, rows):
    if even:
        plane = 0.125 * (read(-1) + read(1)) + 0.75 * read(0)
    else:
        plane = 0.5 * (read(0) + read(1))
    tu_ref[0 : plane.shape[0], :] = plane
    low, mid, high = (tu_ref[k : k + rows, :] for k in range(3))
    z_ref[slot, pl.ds(0, rows, stride=2), :] = 0.125 * (low + high) + 0.75 * mid
    z_ref[slot, pl.ds(1, rows, stride=2), :] = 0.5 * (mid + high)


def spread_mask(column, rows):
    return jnp.broadcast_to(column, (rows, LANES))


UB0, VB0, V0 = 14, 16, 64


def fill_fine(own, low, high, mask, x_ref, sf_ref, sa_ref):
    parts = ((low, 0, 16), (own, 16, 24), (high, 40, 16))
    for u in range(51):
        for tile in range(2):
            for source, row, rows in parts:
                at = slice(row, row + rows)
                lanes = slice(tile * LANES, (tile + 1) * LANES)
                lane = 2 * u + tile
                active = spread_mask(mask[at, lane : lane + 1], rows)
                if x_ref is not None:
                    x_ref[tile, u, at, :] = active * source[u, :, lanes]
                if 3 <= u < 48:
                    sa_ref[tile, u, at, :] = ALPHA * active
                    sf_ref[tile, u, at, :] = (0.5 * active) * source[51 + u - 3, :, lanes]


def fine_pre(own, low, high, mask, x_out, f1_out, x, sf, sa, l_ref, w_ref, t_ref, tu_ref):
    fill_w(w_ref, 256, 256)
    fill_fine(own, low, high, mask, x, sf, sa)
    sweep(x, sf, sa, l_ref, w_ref, 3, 45, 5, 48)
    sweep(x, sf, sa, l_ref, w_ref, 6, 39, 8, 48)
    sweep(x, sf, sa, l_ref, w_ref, 9, 33, 11, 48)
    for tile in range(2):
        x_out[:, :, tile * LANES : (tile + 1) * LANES] = x[tile, 14:38, 16:40, :]
    rw = restrict_w(256, LANES, 256)
    residual(x, sf, sa, l_ref, w_ref, rw, t_ref, 2.0, 12, 27, 14, 32, 0)
    for j in range(12):
        f1_out[j] = narrow_plane(t_ref, tu_ref, j, 32, 12)


def fine_post(
    own, low, high, mask, x_own, x_low, x_high, e_own, e_low, e_high,
    out, x, sf, sa, l_ref, w_ref, e_ref, tu_ref, z_ref,
):
    fill_w(w_ref, 256, 256)
    fill_fine(own, low, high, mask, None, sf, sa)
    e_ref[:, 0:8, :] = e_low[...]
    e_ref[:, 8:20, :] = e_own[...]
    e_ref[:, 20:28, :] = e_high[...]
    pw = prolong_w(LANES, 256, 256)
    position = lax.axis_index("dir")

    def one(i, even):
        u = 2 * i - 10 + (0 if even else 1)
        coarse = i + 1

        def read(k):
            at = coarse + k
            place = 12 * position + at - 6
            inside = jnp.logical_and(place >= 0, place < 48)
            return jnp.where(inside, e_ref[at, 2:26, :], 0.0)

        widen(read, even, tu_ref, z_ref, 0, 22)
        fine = dot_split(z_ref[0, 0:48, :], pw)
        at = u + UB0
        for tile in range(2):
            lanes = slice(tile * LANES, (tile + 1) * LANES)
            x[tile, at, 6:50, :] = fine[0:44, lanes]

    for i in range(22):
        for even in (True, False):
            u = 2 * i - 10 + (0 if even else 1)
            if -9 <= u <= 32:
                one(i, even)
    for u in range(42):
        for tile in range(2):
            lanes = slice(tile * LANES, (tile + 1) * LANES)
            at = u + 5
            for source, row, rows in ((x_low, 0, 16), (x_own, 16, 24), (x_high, 40, 16)):
                part = slice(row, row + rows)
                active = spread_mask(mask[part, 2 * at + tile : 2 * at + tile + 1], rows)
                x[tile, at, part, :] = active * (x[tile, at, part, :] + source[u, :, lanes])
    sweep(x, sf, sa, l_ref, w_ref, 8, 36, 10, 48)
    sweep(x, sf, sa, l_ref, w_ref, 11, 30, 13, 32)
    sweep(x, sf, sa, l_ref, w_ref, 14, 24, 16, 32)
    for tile in range(2):
        out[:, :, tile * LANES : (tile + 1) * LANES] = x[tile, 14:38, 16:40, :]


def fill_next(own, low, high, mask, x_ref, sf_ref, sa_ref):
    for u in range(36):
        for source, row in ((low, 0), (own, 12), (high, 24)):
            at = slice(row, row + 12)
            active = spread_mask(mask[at, u : u + 1], 12)
            value = (0.25 * active) * source[u]
            sa_ref[0, u, at, :] = ALPHA * active
            sf_ref[0, u, at, :] = value
            if x_ref is not None:
                x_ref[0, u, at, :] = value


def next_pre(own, low, high, mask, x_out, f2_out, x, sf, sa, l_ref, w_ref, t_ref, tu_ref):
    fill_w(w_ref, 128, 128)
    fill_next(own, low, high, mask, x, sf, sa)
    sweep(x, sf, sa, l_ref, w_ref, 4, 27, 4, 32)
    sweep(x, sf, sa, l_ref, w_ref, 7, 21, 7, 32)
    x_out[...] = x[0, 12:24, 12:24, :]
    rw = restrict_w(LANES, LANES, 128)
    residual(x, sf, sa, l_ref, w_ref, rw, t_ref, 4.0, 10, 15, 10, 16, 0)
    for j in range(3):
        even = narrow_plane(t_ref, tu_ref, 2 * j, 16, 6)
        odd = narrow_plane(t_ref, tu_ref, 2 * j + 1, 16, 6)
        f2_out[6 * j : 6 * j + 6, :] = even + pltpu.roll(odd, 64, 1)


def next_post(
    own, low, high, mask, x_own, x_low, x_high, e2,
    out, x, sf, sa, l_ref, w_ref, tu_ref, z_ref,
):
    fill_w(w_ref, 128, 128)
    fill_next(own, low, high, mask, None, sf, sa)
    for u in range(36):
        for source, row in ((x_low, 0), (x_own, 12), (x_high, 24)):
            x[0, u, row : row + 12, :] = source[u]
    pw = prolong_w(LANES, LANES, 128)
    for u in range(-9, 21):
        coarse = u // 2 + 5

        def read(k):
            return e2[coarse + k, 0:24, :]

        widen(read, u % 2 == 0, tu_ref, z_ref, 0, 16)
        first = 0.5 * (tu_ref[0:1, :] + tu_ref[1:2, :])
        fine = dot_split(z_ref[0, 0:32, :], pw)
        ahead = dot_split(jnp.broadcast_to(first, (16, LANES)), pw)
        x[0, u + 12, 4:36, :] = x[0, u + 12, 4:36, :] + fine
        x[0, u + 12, 3:4, :] = x[0, u + 12, 3:4, :] + ahead[0:1]
    for u in range(3, 33):
        for row in range(0, 36, 12):
            at = slice(row, row + 12)
            active = spread_mask(mask[at, u : u + 1], 12)
            x[0, u, at, :] = active * x[0, u, at, :]
    sweep(x, sf, sa, l_ref, w_ref, 6, 24, 6, 32)
    sweep(x, sf, sa, l_ref, w_ref, 9, 18, 9, 32)
    sweep(x, sf, sa, l_ref, w_ref, 12, 12, 12, 16)
    out[...] = x[0, 12:24, 12:24, :]


def coarse(same, other, e_out, x, sf, l_ref, w_ref, t_ref, tu_ref, x3, sf3, w3_ref, b_ref, z_ref):
    fill_w(w_ref, 128, 64, True)
    fill_w(w3_ref, 128, 32, True)
    pair, core = lax.axis_index("pz"), lax.axis_index("core")
    position = lax.axis_index("dir")

    for edge in (0, 1, 14, 15):
        x[0, edge] = jnp.zeros(x.shape[2:], F32)
    for edge in (0, 13):
        t_ref[edge] = jnp.zeros(t_ref.shape[1:], F32)

    def place(source, offset, row):
        index = lax.rem(pair + 16 + offset, 16)
        for d in range(4):
            for k in range(3):
                value = 0.125 * source[index * 4 + d, 6 * k : 6 * k + 6, :]
                x[0, 3 * d + k + 2, pl.ds(row, 6), :] = value
                sf[0, 3 * d + k + 2, pl.ds(row, 6), :] = value

    def even_patch(k, _):
        place(same, k - 5, 12 * k)

    def odd_patch(k, _):
        place(other, k - 5 + core, 12 * k + 6)

    lax.fori_loop(0, 11, even_patch, None)
    lax.fori_loop(0, 10, odd_patch, None)

    def smooth(u0, nu, values, loads, factors, v0, nv):
        sweep(values, loads, ALPHA, l_ref, factors, u0, nu, v0, nv, stencil_pairs)

    smooth(2, 12, x, sf, w_ref, 6, 128)
    smooth(2, 12, x, sf, w_ref, 9, 112)
    rw = restrict_w(LANES, LANES, 64, True)
    residual(
        x, sf, ALPHA, l_ref, w_ref, rw, t_ref, 8.0, 2, 12, 12, 112, 1, stencil_pairs
    )

    for edge in (0, 1, 8, 9):
        x3[0, edge] = jnp.zeros(x3.shape[2:], F32)

    def low_half(rows):
        return lax.broadcasted_iota(jnp.int32, (rows, LANES), 1) < 64

    def narrow(m, _):
        parts = []
        for odd in (0, 1):
            j = 2 * m + odd
            before, own, after = (t_ref[j + i, 0:112, :] for i in range(3))
            value = jnp.where(
                low_half(112), 0.125 * (before + after) + 0.75 * own, 0.5 * (before + own)
            )
            parts.append(value + pltpu.roll(value, 64, 1))
        tu_ref[0:112, :] = jnp.where(low_half(112), parts[0], parts[1])
        at = [tu_ref[pl.ds(i, 50, stride=2), :] for i in range(5)]
        value = 0.0625 * (0.125 * (at[0] + at[4]) + 0.5 * (at[1] + at[3]) + 0.75 * at[2])
        x3[0, m + 2, 3:53, :] = value
        sf3[0, m + 2, 3:53, :] = value

    lax.fori_loop(0, 6, narrow, None)
    smooth(2, 6, x3, sf3, w3_ref, 6, 48)
    smooth(2, 6, x3, sf3, w3_ref, 9, 48)
    smooth(2, 6, x3, sf3, w3_ref, 12, 32)
    smooth(2, 6, x3, sf3, w3_ref, 15, 32)
    smooth(2, 6, x3, sf3, w3_ref, 18, 32)

    pw = prolong_w(LANES, LANES, 64, True)
    for edge in (0, 13):
        b_ref[edge] = jnp.zeros(b_ref.shape[1:], F32)
    for m in range(6):
        value = x3[0, m + 2, 18:42, :]
        turned = pltpu.roll(value, 64, 1)
        b_ref[2 * m + 1] = jnp.where(low_half(24), value, turned)
        b_ref[2 * m + 2] = jnp.where(low_half(24), turned, value)

    def wide(k, _):
        before, own, after = (b_ref[k + i] for i in range(3))
        tu_ref[0:24, :] = jnp.where(
            low_half(24), 0.125 * (before + after) + 0.75 * own, 0.5 * (own + after)
        )
        first, mid, last = (tu_ref[i : i + 22, :] for i in range(3))
        z_ref[0, pl.ds(0, 22, stride=2), :] = 0.125 * (first + last) + 0.75 * mid
        z_ref[0, pl.ds(1, 22, stride=2), :] = 0.5 * (mid + last)
        fine = dot_split(z_ref[0, 0:48, :], pw)
        at = (0, k + 2, slice(46, 94), slice(None))
        x[at] = x[at] + fine

    lax.fori_loop(0, 12, wide, None)
    smooth(2, 12, x, sf, w_ref, 49, 32)
    smooth(2, 12, x, sf, w_ref, 52, 32)
    smooth(2, 12, x, sf, w_ref, 55, 32)

    for k in range(17):
        index = 3 * position + (k - 5) // 2
        inside = jnp.logical_and(index >= 0, index < 12)
        value = x[0, jnp.clip(index, 0, 11) + 2, 55:79, :]
        if k % 2 == 0:
            value = pltpu.roll(value, 64, 1)
        e_out[k] = jnp.where(inside & low_half(24), value, 0.0)


def call(body, outs, scratch, operands, flops):
    vmem = pl.BlockSpec(memory_space=pltpu.VMEM)
    size = 0
    for array in list(operands) + list(outs):
        dims = list(array.shape)
        dims[-1] = -(-dims[-1] // 128) * 128
        dims[-2] = -(-dims[-2] // 16) * 16
        count = 1
        for dim in dims:
            count *= dim
        size += 4 * count
    for shape, kind in scratch:
        count = 1
        for dim in shape:
            count *= dim
        size += count * (2 if kind == BF16 else 4)
    return pl.pallas_call(
        body,
        out_shape=list(outs),
        in_specs=[vmem] * len(operands),
        out_specs=[vmem] * len(outs),
        scratch_shapes=[pltpu.VMEM(shape, kind) for shape, kind in scratch],
        compiler_params=pltpu.CompilerParams(vmem_limit_bytes=size + (6 << 20)),
        cost_estimate=pl.CostEstimate(flops=flops, bytes_accessed=size, transcendentals=0),
    )(*operands)


def shape_of(*dims):
    return jax.ShapeDtypeStruct(dims, F32)


def ring(value, axes, step):
    count = 1
    for axis in axes:
        count *= lax.axis_size(axis)
    pairs = [(i, (i + step) % count) for i in range(count)]
    return lax.ppermute(value, axes if len(axes) > 1 else axes[0], pairs)


def along_dir(value, before, after):
    count = value.shape[0]
    low = ring(value[count - before :], ("dir",), 1)
    high = ring(value[:after], ("dir",), -1)
    return low, high


def along_next(value):
    low, high = along_dir(value, 12, 12)
    return jnp.concatenate([low, value, high], axis=0)


def along_patch(value, low_rows, high_rows):
    low = ring(value[:, low_rows[0] : low_rows[1]], PATCH, 1)
    high = ring(value[:, high_rows[0] : high_rows[1]], PATCH, -1)
    return low, high


def after(value, other):
    return lax.optimization_barrier((value, other))


def inside_lanes(first, count, per, total):
    plane = first + jnp.arange(count) // per
    return ((plane >= 0) & (plane < total)).astype(F32)


def on_device(right_side, guess, mask_fine, mask_next):
    position = lax.axis_index("dir")
    fine = jnp.transpose(mask_fine, (1, 0, 2)).reshape(24, 48).astype(F32)
    following = mask_next[:, :, 0].T.astype(F32)
    plane = jnp.concatenate(
        [
            jnp.pad(fine, ((0, 0), (0, 80))),
            jnp.pad(following, ((0, 12), (0, 116))),
        ],
        axis=1,
    )[None]
    up = jnp.concatenate([guess[10:], right_side[13:], plane], axis=0)
    down = jnp.concatenate([guess[:13], right_side[:10], plane], axis=0)
    low = ring(up, ("dir",), 1)
    high = ring(down, ("dir",), -1)
    m_low, m_high, m_own = low[25], high[23], plane[0]
    fine = jnp.concatenate([m_low[:, 20:48], m_own[:, :48], m_high[:, :26]], axis=1)
    fine = fine * inside_lanes(24 * position - 14, 102, 2, 96)
    following = jnp.concatenate(
        [m_low[:12, 128:140], m_own[:12, 128:140], m_high[:12, 128:140]], axis=1
    )
    following = following * inside_lanes(12 * position - 12, 36, 1, 48)
    plane = jnp.concatenate(
        [
            jnp.pad(fine, ((0, 0), (0, 26))),
            jnp.pad(following, ((12, 0), (0, 28))) + jnp.zeros((24, 64), F32),
            jnp.pad(following, ((0, 12), (0, 28))) + jnp.zeros((24, 64), F32),
        ],
        axis=1,
    )[None]
    own = jnp.concatenate(
        [low[:14], guess, high[:13], low[14:25], right_side, high[13:23], plane], axis=0
    )
    low = ring(own[:, 8:24], PATCH, 1)
    high = ring(own[:, 0:16], PATCH, -1)
    mask0 = jnp.concatenate([low[96, :, :128], own[96, :, :128], high[96, :, :128]], axis=0)
    mask1 = jnp.concatenate(
        [low[96, 4:16, 128:192], own[96, 12:24, 128:192], high[96, 0:12, 192:256]], axis=0
    )
    mask1 = jnp.pad(mask1, ((0, 4), (0, 64)))

    window = ((2, 52, V0, LANES), F32)
    left0 = ((46, 48, 1024), BF16)
    w0 = ((1280, 256), BF16)
    x0, f1 = call(
        fine_pre,
        [shape_of(24, 24, 256), shape_of(12, 12, 128)],
        [window, window, window, left0, w0, ((28, 32, 128), F32), ((48, 128), F32)],
        (own, low, high, mask0),
        10**10,
    )

    f1_own = along_next(f1)
    x0, f1_own = after(x0, f1_own)
    f1_low, f1_high = along_patch(f1_own, (0, 12), (0, 12))
    window1 = ((1, 36, 48, LANES), F32)
    left1 = ((28, 32, 512), BF16)
    w1 = ((640, 128), BF16)
    x1, f2 = call(
        next_pre,
        [shape_of(12, 12, 128), shape_of(18, 128)],
        [window1, window1, window1, left1, w1, ((16, 16, 128), F32), ((48, 128), F32)],
        (f1_own, f1_low, f1_high, mask1),
        10**9,
    )

    x0_low, x0_high = along_dir(x0, 9, 9)
    x0_own = jnp.concatenate([x0_low, x0, x0_high], axis=0)
    x0_own, f2 = after(x0_own, f2)
    x0_low, x0_high = along_patch(x0_own, (8, 24), (0, 16))
    x1_own = along_next(x1)

    same = lax.all_to_all(jnp.broadcast_to(f2[None], (64, 18, 128)), ("pz", "dir"), 0, 0)
    x1_own, same = after(x1_own, same)
    other = lax.ppermute(same, "core", [(0, 1), (1, 0)])
    x1_low, x1_high = along_patch(x1_own, (0, 12), (0, 12))
    (e2,) = call(
        coarse,
        [shape_of(17, 24, 128)],
        [
            ((1, 16, 144, LANES), F32),
            ((1, 16, 144, LANES), F32),
            ((12, 128, 512), BF16),
            w1,
            ((14, 112, 128), F32),
            ((112, 128), F32),
            ((1, 10, 64, LANES), F32),
            ((1, 10, 64, LANES), F32),
            w1,
            ((14, 24, 128), F32),
            ((2, 48, 128), F32),
        ],
        (same, other),
        4 * 10**9,
    )
    (e1,) = call(
        next_post,
        [shape_of(12, 12, 128)],
        [window1, window1, window1, left1, w1, ((48, 128), F32), ((2, 48, 128), F32)],
        (f1_own, f1_low, f1_high, mask1, x1_own, x1_low, x1_high, e2),
        10**9,
    )
    e1_low, e1_high = along_dir(e1, 6, 6)
    e1_own = jnp.concatenate([e1_low, e1, e1_high], axis=0)
    e1_low = ring(e1_own[:, 4:12], PATCH, 1)
    e1_high = ring(e1_own[:, 0:8], PATCH, -1)
    (out,) = call(
        fine_post,
        [shape_of(24, 24, 256)],
        [
            window,
            window,
            window,
            left0,
            w0,
            ((24, 32, 128), F32),
            ((48, 128), F32),
            ((2, 48, 128), F32),
        ],
        (own, low, high, mask0, x0_own, x0_low, x0_high, e1_own, e1_low, e1_high),
        10**10,
    )
    return out


def solution(mesh):
    pairs = Mesh(mesh.devices.reshape(16, 2, 4), ("pz", "core", "dir"))
    spec = P("dir", PATCH, None)
    return jax.shard_map(
        on_device, mesh=pairs, in_specs=(spec,) * 4, out_specs=spec, check_vma=False
    )
```

```python
import functools

import jax
import jax.numpy as jnp
from jax import lax
from jax.experimental import pallas as pl
from jax.experimental.pallas import tpu as pltpu
from jax.sharding import Mesh
from jax.sharding import PartitionSpec as P

F32 = jnp.float32
BF16 = jnp.bfloat16
LANES = 128

MASS = (2416.0, 1191.0, 120.0, 1.0)
STIFF = (80.0, -15.0, -24.0, -1.0)
ALPHA = 0.5 / (120.0 * 5040.0 * 5040.0)
PATCH = ("pz", "core")


def dot(a, b):
    return jnp.dot(a, b, preferred_element_type=F32)


def split(value):
    high = value.astype(BF16)
    return high, (value - high.astype(F32)).astype(BF16)


def dot_split(value, matrix):
    high, low = split(value)
    return dot(high, matrix) + dot(low, matrix)


def banded(rows, columns, size_r, size_c, coeffs, row_step, column_step, pairs=False):
    i = lax.broadcasted_iota(jnp.int32, (rows, columns), 0)
    j = lax.broadcasted_iota(jnp.int32, (rows, columns), 1)
    same = i >= 0
    if pairs:
        same = (i < 64) == (j < 64)
        i, j = jnp.where(i < 64, i, i - 64), jnp.where(j < 64, j, j - 64)
    at = row_step * i + column_step * j
    out = jnp.zeros((rows, columns), F32)
    for key, weight in coeffs.items():
        out = jnp.where(at == key, weight, out)
    return jnp.where((i < size_r) & (j < size_c) & same, out, 0.0).astype(BF16)


def fill_w(w_ref, depth, size, pairs=False):
    mass = {0: 2416.0, 1: 1192.0, -1: 1192.0, 2: 120.0, -2: 120.0, 3: 1.0, -3: 1.0}
    low = {1: -1.0, -1: -1.0}
    stiff = {0: 80.0, 1: -15.0, -1: -15.0, 2: -24.0, -2: -24.0, 3: -1.0, -3: -1.0}
    for block, table in enumerate((mass, mass, stiff, stiff, low)):
        w_ref[block * depth : (block + 1) * depth, :] = banded(
            depth, depth, size, size, table, 1, -1, pairs
        )


def restrict_w(rows, columns, size, pairs=False):
    taps = {-2: 0.125, -1: 0.5, 0: 0.75, 1: 0.5, 2: 0.125}
    return banded(rows, columns, size, size // 2, taps, 1, -2, pairs)


def prolong_w(rows, columns, size, pairs=False):
    taps = {-2: 0.125, -1: 0.5, 0: 0.75, 1: 0.5, 2: 0.125}
    return banded(rows, columns, size // 2, size, taps, -2, 1, pairs)


def stencil(x_ref, l_ref, u0, nu, v0, nv):
    tiles = x_ref.shape[0]
    depth = tiles * LANES

    def weigh(centre, one, two, three, taps):
        return taps[0] * centre + taps[1] * one + taps[2] * two + taps[3] * three

    for tile in range(tiles):
        for column in range(nv // 16):
            row = v0 + 16 * column

            def plane(u):
                x = [x_ref[tile, u, pl.ds(row - 3 + k, 16), :] for k in range(7)]
                one, two, three = x[2] + x[4], x[1] + x[5], x[0] + x[6]
                p = 2416.0 * x[3] + 1191.0 * one + 120.0 * two + three
                q = 80.0 * x[3] - 15.0 * one - 24.0 * two - three
                return p, q

            def emit(at, ps, qs):
                p1, p2, p3 = ps[2] + ps[4], ps[1] + ps[5], ps[0] + ps[6]
                q1, q2, q3 = qs[2] + qs[4], qs[1] + qs[5], qs[0] + qs[6]
                r = 2416.0 * ps[3] + 1191.0 * p1 + 120.0 * p2 + p3
                s = (80.0 * ps[3] - 15.0 * p1 - 24.0 * p2 - p3) + (
                    2416.0 * qs[3] + 1191.0 * q1 + 120.0 * q2 + q3
                )
                for part, value in enumerate(split(s) + split(r)):
                    lane = part * depth + tile * LANES
                    l_ref[at, 16 * column : 16 * column + 16, lane : lane + LANES] = value

            def several(first, count, carry):
                ps, qs = list(carry[:6]), list(carry[6:])
                for k in range(count):
                    p, q = plane(u0 + first + k + 3)
                    emit(first + k, ps + [p], qs + [q])
                    ps, qs = ps[1:] + [p], qs[1:] + [q]
                return tuple(ps + qs)

            start = [plane(u0 - 3 + k) for k in range(6)]
            carry = tuple([p for p, _ in start] + [q for _, q in start])
            groups = nu // 6
            if groups > 1:
                carry = lax.fori_loop(0, groups, lambda g, c: several(6 * g, 6, c), carry)
            elif groups == 1:
                carry = several(0, 6, carry)
            if nu % 6:
                several(6 * groups, nu % 6, carry)


def stencil_pairs(x_ref, l_ref, k0, nk, v0, nv):
    low = lax.broadcasted_iota(jnp.int32, (16, LANES), 1) < 64

    for column in range(nv // 16):
        row = v0 + 16 * column

        def plane(k):
            x = [x_ref[0, k, pl.ds(row - 3 + i, 16), :] for i in range(7)]
            one, two, three = x[2] + x[4], x[1] + x[5], x[0] + x[6]
            p = 2416.0 * x[3] + 1191.0 * one + 120.0 * two + three
            q = 80.0 * x[3] - 15.0 * one - 24.0 * two - three
            return p, pltpu.roll(p, 64, 1), q, pltpu.roll(q, 64, 1)

        def sums(own, other):
            one = other[2] + jnp.where(low, other[1], other[3])
            three = jnp.where(low, other[0], other[4]) + jnp.where(low, other[3], other[1])
            return own[2], one, own[1] + own[3], three

        def emit(at, planes):
            p, p1, p2, p3 = sums([t[0] for t in planes], [t[1] for t in planes])
            q, q1, q2, q3 = sums([t[2] for t in planes], [t[3] for t in planes])
            r = 2416.0 * p + 1191.0 * p1 + 120.0 * p2 + p3
            s = (80.0 * p - 15.0 * p1 - 24.0 * p2 - p3) + (
                2416.0 * q + 1191.0 * q1 + 120.0 * q2 + q3
            )
            for part, value in enumerate(split(s) + split(r)):
                l_ref[at, 16 * column : 16 * column + 16, part * LANES : (part + 1) * LANES] = value

        def several(first, count, carry):
            planes = [carry[4 * i : 4 * i + 4] for i in range(4)]
            for i in range(count):
                planes = planes + [plane(k0 + first + i + 2)]
                emit(first + i, planes)
                planes = planes[1:]
            return tuple(value for t in planes for value in t)

        carry = tuple(value for i in range(4) for value in plane(k0 - 2 + i))
        if nk > 6:
            lax.fori_loop(0, nk // 4, lambda g, c: several(4 * g, 4, c), carry)
        else:
            several(0, nk, carry)


def finish(l_ref, w_ref, nu, nv, use):
    depth = w_ref.shape[1]
    chunk = max(1, min(nu, 384 // nv))

    def some(first, count):
        left = l_ref[pl.ds(first, count), 0:nv, :].reshape(count * nv, 4 * depth)
        use(
            first,
            count,
            dot(left, w_ref[0 : 4 * depth, :])
            + dot(left[:, 0:depth], w_ref[4 * depth : 5 * depth, :]),
        )

    whole = nu // chunk
    if whole > 1:
        lax.fori_loop(0, whole, lambda c, _: some(c * chunk, chunk), None)
    elif whole == 1:
        some(0, chunk)
    if nu % chunk:
        some(whole * chunk, nu % chunk)


def sweep(x_ref, sf_ref, sa, l_ref, w_ref, u0, nu, v0, nv, apply=stencil):
    apply(x_ref, l_ref, u0, nu, v0, nv)

    def use(first, count, product):
        for tile in range(x_ref.shape[0]):
            at = (tile, pl.ds(u0 + first, count), pl.ds(v0, nv), slice(None))
            part = product[:, tile * LANES : (tile + 1) * LANES].reshape(count, nv, LANES)
            weight = sa if isinstance(sa, float) else sa[at]
            x_ref[at] = x_ref[at] + (sf_ref[at] - weight * part)

    finish(l_ref, w_ref, nu, nv, use)


def residual(x_ref, sf_ref, sa, l_ref, w_ref, rw, t_ref, scale, u0, nu, v0, nv, t0, apply=stencil):
    apply(x_ref, l_ref, u0, nu, v0, nv)

    def use(first, count, product):
        parts = []
        for tile in range(x_ref.shape[0]):
            at = (tile, pl.ds(u0 + first, count), pl.ds(v0, nv), slice(None))
            part = product[:, tile * LANES : (tile + 1) * LANES].reshape(count, nv, LANES)
            weight = sa if isinstance(sa, float) else sa[at]
            value = scale * (sf_ref[at] - weight * part)
            parts.append(value.reshape(count * nv, LANES))
        whole = parts[0] if len(parts) == 1 else jnp.concatenate(parts, axis=1)
        narrow = dot_split(whole, rw)
        t_ref[pl.ds(t0 + first, count), 0:nv, :] = narrow.reshape(count, nv, LANES)

    finish(l_ref, w_ref, nu, nv, use)


def narrow_plane(t_ref, tu_ref, j, nv, rows):
    at = [t_ref[2 * j + k, 0:nv, :] for k in range(5)]
    tu_ref[0:nv, :] = 0.125 * (at[0] + at[4]) + 0.5 * (at[1] + at[3]) + 0.75 * at[2]
    at = [tu_ref[pl.ds(k, rows, stride=2), :] for k in range(5)]
    return 0.125 * (at[0] + at[4]) + 0.5 * (at[1] + at[3]) + 0.75 * at[2]


def widen(read, even, tu_ref, z_ref, slot, rows):
    if even:
        plane = 0.125 * (read(-1) + read(1)) + 0.75 * read(0)
    else:
        plane = 0.5 * (read(0) + read(1))
    tu_ref[0 : plane.shape[0], :] = plane
    low, mid, high = (tu_ref[k : k + rows, :] for k in range(3))
    z_ref[slot, pl.ds(0, rows, stride=2), :] = 0.125 * (low + high) + 0.75 * mid
    z_ref[slot, pl.ds(1, rows, stride=2), :] = 0.5 * (mid + high)


def spread_mask(column, rows):
    return jnp.broadcast_to(column, (rows, LANES))


UB0, VB0, V0 = 14, 16, 64

UP_X, UP_F, DOWN_X, DOWN_F = 14, 11, 13, 10
UP_AT = (0, 102 * UP_X, 102 * UP_X + 90 * UP_F)
DOWN_AT = (0, 102 * DOWN_X, 102 * DOWN_X + 90 * DOWN_F)
UP_ROWS = 2448
DOWN_ROWS = 2256


def pack_dir(guess, load, up, down, sems):
    copies = [
        pltpu.make_async_copy(guess.at[10:24], up.at[0:14], sems.at[0]),
        pltpu.make_async_copy(load.at[13:24], up.at[14:25], sems.at[1]),
        pltpu.make_async_copy(guess.at[0:13], down.at[0:13], sems.at[2]),
        pltpu.make_async_copy(load.at[0:10], down.at[13:23], sems.at[3]),
    ]
    for copy in copies:
        copy.start()
    for copy in copies:
        copy.wait()


def x_plane(low, guess, high, u):
    if u < 14:
        return low.at[u]
    return guess.at[u - 14] if u < 38 else high.at[u - 38]


def f_plane(low, load, high, u):
    if u < 11:
        return low.at[14 + u]
    return load.at[u - 11] if u < 35 else high.at[13 + u - 35]


def pack_patch(guess, load, low, high, plane, up, down):
    def put(source, at, tile, index, rows, target, top):
        lanes = slice(tile * LANES, (tile + 1) * LANES)
        first = 24 - rows if top else 0
        row = at + (2 * index + tile) * rows
        target[row : row + rows, :] = source[first : first + rows, lanes]

    for u in range(51):
        for tile in range(2):
            source = x_plane(low, guess, high, u)
            put(source, UP_AT[0], tile, u, UP_X, up, True)
            put(source, DOWN_AT[0], tile, u, DOWN_X, down, False)
    for u in range(45):
        for tile in range(2):
            source = f_plane(low, load, high, u)
            put(source, UP_AT[1], tile, u, UP_F, up, True)
            put(source, DOWN_AT[1], tile, u, DOWN_F, down, False)
    at = UP_AT[2]
    up[at : at + 14, :] = plane[10:24, 0:LANES]
    up[at + 14 : at + 26, :] = plane[0:12, LANES:]
    at = DOWN_AT[2]
    down[at : at + 13, :] = plane[0:13, 0:LANES]
    down[at + 13 : at + 25, :] = plane[0:12, LANES:]


def fill_fine(pieces, m_ref, x_ref, sf_ref, sa_ref):
    guess, load, low, high, up, down, plane = pieces
    m_ref[2:16, :] = up[UP_AT[2] : UP_AT[2] + 14, :]
    m_ref[16:40, :] = plane[:, 0:LANES]
    m_ref[40:53, :] = down[DOWN_AT[2] : DOWN_AT[2] + 13, :]
    for u in range(51):
        for tile in range(2):
            lanes = slice(tile * LANES, (tile + 1) * LANES)
            lane = slice(2 * u + tile, 2 * u + tile + 1)
            if x_ref is not None:
                source = x_plane(low, guess, high, u)
                index = 2 * u + tile
                row = UP_AT[0] + index * UP_X
                x_ref[tile, u, 2:16, :] = up[row : row + 14, :] * spread_mask(m_ref[2:16, lane], 14)
                x_ref[tile, u, 16:40, :] = source[:, lanes] * spread_mask(m_ref[16:40, lane], 24)
                row = DOWN_AT[0] + index * DOWN_X
                x_ref[tile, u, 40:53, :] = down[row : row + 13, :] * spread_mask(
                    m_ref[40:53, lane], 13
                )
            if 3 <= u < 48:
                source = f_plane(low, load, high, u - 3)
                index = 2 * (u - 3) + tile
                row = UP_AT[1] + index * UP_F
                active = spread_mask(m_ref[5:16, lane], 11)
                sa_ref[tile, u, 5:16, :] = ALPHA * active
                sf_ref[tile, u, 5:16, :] = (0.5 * active) * up[row : row + 11, :]
                active = spread_mask(m_ref[16:40, lane], 24)
                sa_ref[tile, u, 16:40, :] = ALPHA * active
                sf_ref[tile, u, 16:40, :] = (0.5 * active) * source[:, lanes]
                row = DOWN_AT[1] + index * DOWN_F
                active = spread_mask(m_ref[40:50, lane], 10)
                sa_ref[tile, u, 40:50, :] = ALPHA * active
                sf_ref[tile, u, 40:50, :] = (0.5 * active) * down[row : row + 10, :]


def fine_pre(
    guess, load, low, high, up, down, plane,
    x_out, f1_out, mask_out, x, sf, sa, l_ref, w_ref, t_ref, tu_ref, m_ref,
):
    fill_w(w_ref, 256, 256)
    fill_fine((guess, load, low, high, up, down, plane), m_ref, x, sf, sa)
    mask_out[0:12, :] = up[UP_AT[2] + 14 : UP_AT[2] + 26, :]
    mask_out[12:24, :] = plane[0:12, LANES:]
    mask_out[24:36, :] = down[DOWN_AT[2] + 13 : DOWN_AT[2] + 25, :]
    mask_out[36:40, :] = jnp.zeros((4, LANES), F32)
    sweep(x, sf, sa, l_ref, w_ref, 3, 45, 5, 48)
    sweep(x, sf, sa, l_ref, w_ref, 6, 39, 8, 48)
    sweep(x, sf, sa, l_ref, w_ref, 9, 33, 11, 48)
    for tile in range(2):
        x_out[:, :, tile * LANES : (tile + 1) * LANES] = x[tile, 14:38, 16:40, :]
    rw = restrict_w(256, LANES, 256)
    residual(x, sf, sa, l_ref, w_ref, rw, t_ref, 2.0, 12, 27, 14, 32, 0)
    for j in range(12):
        f1_out[j] = narrow_plane(t_ref, tu_ref, j, 32, 12)


def fine_post(
    guess, load, low, high, up, down, plane, x_own, x_low, x_high,
    f1_own, f1_low, f1_high, mask1, y_own, y_low, y_high,
    out, x, sf, sa, l_ref, w_ref, tu_ref, z_ref, m_ref, y, sf1, sa1, l1_ref, w1_ref,
):
    fill_w(w_ref, 256, 256)
    fill_fine((guess, load, low, high, up, down, plane), m_ref, None, sf, sa)

    fill_w(w1_ref, 128, 128)
    fill_next(f1_own, f1_low, f1_high, mask1, None, sf1, sa1)
    for u in range(30):
        for source, row, rows in ((y_low, 4, 8), (y_own, 12, 12), (y_high, 24, 9)):
            part = slice(row, row + rows)
            active = spread_mask(mask1[part, u + 3 : u + 4], rows)
            y[0, u + 3, part, :] = active * source[u]
    sweep(y, sf1, sa1, l1_ref, w1_ref, 7, 23, 7, 32)

    pw = prolong_w(LANES, 256, 256)
    for u in range(-9, 33):

        def read(k):
            return y[0, u // 2 + 12 + k, 6:30, :]

        widen(read, u % 2 == 0, tu_ref, z_ref, 0, 22)
        fine = dot_split(z_ref[0, 0:48, :], pw)
        for tile in range(2):
            lanes = slice(tile * LANES, (tile + 1) * LANES)
            x[tile, u + UB0, 6:50, :] = fine[0:44, lanes]
    for u in range(42):
        for tile in range(2):
            lanes = slice(tile * LANES, (tile + 1) * LANES)
            at = u + 5
            for source, row, rows, first in (
                (x_low, 7, 9, 7), (x_own, 16, 24, 0), (x_high, 40, 9, 0)
            ):
                part = slice(row, row + rows)
                active = spread_mask(m_ref[part, 2 * at + tile : 2 * at + tile + 1], rows)
                x[tile, at, part, :] = active * (
                    x[tile, at, part, :] + source[u, first : first + rows, lanes]
                )
    sweep(x, sf, sa, l_ref, w_ref, 8, 36, 10, 48)
    sweep(x, sf, sa, l_ref, w_ref, 11, 30, 13, 32)
    sweep(x, sf, sa, l_ref, w_ref, 14, 24, 16, 32)
    for tile in range(2):
        out[:, :, tile * LANES : (tile + 1) * LANES] = x[tile, 14:38, 16:40, :]


def fill_next(own, low, high, mask, x_ref, sf_ref, sa_ref):
    for u in range(36):
        for source, row in ((low, 0), (own, 12), (high, 24)):
            at = slice(row, row + 12)
            active = spread_mask(mask[at, u : u + 1], 12)
            value = (0.25 * active) * source[u]
            sa_ref[0, u, at, :] = ALPHA * active
            sf_ref[0, u, at, :] = value
            if x_ref is not None:
                x_ref[0, u, at, :] = value


def next_pre(own, low, high, mask, x_out, f2_out, x, sf, sa, l_ref, w_ref, t_ref, tu_ref):
    fill_w(w_ref, 128, 128)
    fill_next(own, low, high, mask, x, sf, sa)
    sweep(x, sf, sa, l_ref, w_ref, 3, 30, 3, 32)
    sweep(x, sf, sa, l_ref, w_ref, 6, 24, 6, 32)
    x_out[...] = x[0, 6:30, 6:30, :]
    rw = restrict_w(LANES, LANES, 128)
    residual(x, sf, sa, l_ref, w_ref, rw, t_ref, 4.0, 10, 15, 10, 16, 0)
    for j in range(3):
        even = narrow_plane(t_ref, tu_ref, 2 * j, 16, 6)
        odd = narrow_plane(t_ref, tu_ref, 2 * j + 1, 16, 6)
        tu_ref[24 + 6 * j : 30 + 6 * j, :] = even + pltpu.roll(odd, 64, 1)
    value = tu_ref[24:42, :]
    for peer in range(64):
        f2_out[peer] = value


def next_post(
    own, low, high, mask, x_own, e2,
    out, x, sf, sa, l_ref, w_ref, tu_ref, z_ref,
):
    fill_w(w_ref, 128, 128)
    fill_next(own, low, high, mask, None, sf, sa)
    pw = prolong_w(LANES, LANES, 128)
    for u in range(-6, 18):
        coarse = u // 2 + 5

        def read(k):
            return e2[coarse + k, 0:24, :]

        widen(read, u % 2 == 0, tu_ref, z_ref, 0, 16)
        x[0, u + 12, 4:36, :] = dot_split(z_ref[0, 0:32, :], pw)
    for u in range(6, 30):
        for row in (6, 18):
            at = slice(row, row + 12)
            active = spread_mask(mask[at, u : u + 1], 12)
            x[0, u, at, :] = active * (x[0, u, at, :] + x_own[u - 6, row - 6 : row + 6, :])
    sweep(x, sf, sa, l_ref, w_ref, 9, 18, 9, 32)
    sweep(x, sf, sa, l_ref, w_ref, 12, 12, 12, 16)
    out[...] = x[0, 12:24, 12:24, :]


def coarse(same, other, e_out, x, sf, l_ref, w_ref, t_ref, tu_ref, x3, sf3, w3_ref, b_ref, z_ref):
    fill_w(w_ref, 128, 64, True)
    fill_w(w3_ref, 128, 32, True)
    pair, core = lax.axis_index("pz"), lax.axis_index("core")
    position = lax.axis_index("dir")

    for edge in (0, 1, 14, 15):
        x[0, edge] = jnp.zeros(x.shape[2:], F32)
    for edge in (0, 13):
        t_ref[edge] = jnp.zeros(t_ref.shape[1:], F32)

    def place(source, offset, row):
        index = lax.rem(pair + 16 + offset, 16)
        for d in range(4):
            for k in range(3):
                value = 0.125 * source[index * 4 + d, 6 * k : 6 * k + 6, :]
                x[0, 3 * d + k + 2, pl.ds(row, 6), :] = value
                sf[0, 3 * d + k + 2, pl.ds(row, 6), :] = value

    def even_patch(k, _):
        place(same, k - 5, 12 * k)

    def odd_patch(k, _):
        place(other, k - 5 + core, 12 * k + 6)

    lax.fori_loop(0, 11, even_patch, None)
    lax.fori_loop(0, 10, odd_patch, None)

    def smooth(u0, nu, values, loads, factors, v0, nv):
        sweep(values, loads, ALPHA, l_ref, factors, u0, nu, v0, nv, stencil_pairs)

    smooth(2, 12, x, sf, w_ref, 6, 128)
    smooth(2, 12, x, sf, w_ref, 9, 112)
    rw = restrict_w(LANES, LANES, 64, True)
    residual(
        x, sf, ALPHA, l_ref, w_ref, rw, t_ref, 8.0, 2, 12, 12, 112, 1, stencil_pairs
    )

    for edge in (0, 1, 8, 9):
        x3[0, edge] = jnp.zeros(x3.shape[2:], F32)

    def low_half(rows):
        return lax.broadcasted_iota(jnp.int32, (rows, LANES), 1) < 64

    def narrow(m, _):
        parts = []
        for odd in (0, 1):
            j = 2 * m + odd
            before, own, after = (t_ref[j + i, 0:112, :] for i in range(3))
            value = jnp.where(
                low_half(112), 0.125 * (before + after) + 0.75 * own, 0.5 * (before + own)
            )
            parts.append(value + pltpu.roll(value, 64, 1))
        tu_ref[0:112, :] = jnp.where(low_half(112), parts[0], parts[1])
        at = [tu_ref[pl.ds(i, 50, stride=2), :] for i in range(5)]
        value = 0.0625 * (0.125 * (at[0] + at[4]) + 0.5 * (at[1] + at[3]) + 0.75 * at[2])
        x3[0, m + 2, 3:53, :] = value
        sf3[0, m + 2, 3:53, :] = value

    lax.fori_loop(0, 6, narrow, None)
    smooth(2, 6, x3, sf3, w3_ref, 6, 48)
    smooth(2, 6, x3, sf3, w3_ref, 9, 48)
    smooth(2, 6, x3, sf3, w3_ref, 12, 32)
    smooth(2, 6, x3, sf3, w3_ref, 15, 32)
    smooth(2, 6, x3, sf3, w3_ref, 18, 32)

    pw = prolong_w(LANES, LANES, 64, True)
    for edge in (0, 13):
        b_ref[edge] = jnp.zeros(b_ref.shape[1:], F32)
    for m in range(6):
        value = x3[0, m + 2, 18:42, :]
        turned = pltpu.roll(value, 64, 1)
        b_ref[2 * m + 1] = jnp.where(low_half(24), value, turned)
        b_ref[2 * m + 2] = jnp.where(low_half(24), turned, value)

    def wide(k, _):
        before, own, after = (b_ref[k + i] for i in range(3))
        tu_ref[0:24, :] = jnp.where(
            low_half(24), 0.125 * (before + after) + 0.75 * own, 0.5 * (own + after)
        )
        first, mid, last = (tu_ref[i : i + 22, :] for i in range(3))
        z_ref[0, pl.ds(0, 22, stride=2), :] = 0.125 * (first + last) + 0.75 * mid
        z_ref[0, pl.ds(1, 22, stride=2), :] = 0.5 * (mid + last)
        fine = dot_split(z_ref[0, 0:48, :], pw)
        at = (0, k + 2, slice(46, 94), slice(None))
        x[at] = x[at] + fine

    lax.fori_loop(0, 12, wide, None)
    smooth(2, 12, x, sf, w_ref, 49, 32)
    smooth(2, 12, x, sf, w_ref, 52, 32)
    smooth(2, 12, x, sf, w_ref, 55, 32)

    for k in range(17):
        index = 3 * position + (k - 5) // 2
        inside = jnp.logical_and(index >= 0, index < 12)
        value = x[0, jnp.clip(index, 0, 11) + 2, 55:79, :]
        if k % 2 == 0:
            value = pltpu.roll(value, 64, 1)
        e_out[k] = jnp.where(inside & low_half(24), value, 0.0)


def call(body, outs, scratch, operands, flops):
    vmem = pl.BlockSpec(memory_space=pltpu.VMEM)
    size = 0
    for array in list(operands) + list(outs):
        dims = list(array.shape)
        dims[-1] = -(-dims[-1] // 128) * 128
        dims[-2] = -(-dims[-2] // 16) * 16
        count = 1
        for dim in dims:
            count *= dim
        size += 4 * count
    for shape, kind in scratch:
        count = 1
        for dim in shape:
            count *= dim
        size += count * (2 if kind == BF16 else 4)
    return pl.pallas_call(
        body,
        out_shape=list(outs),
        in_specs=[vmem] * len(operands),
        out_specs=[vmem] * len(outs),
        scratch_shapes=[pltpu.VMEM(shape, kind) for shape, kind in scratch],
        compiler_params=pltpu.CompilerParams(vmem_limit_bytes=size + (6 << 20)),
        cost_estimate=pl.CostEstimate(flops=flops, bytes_accessed=size, transcendentals=0),
    )(*operands)


def shape_of(*dims):
    return jax.ShapeDtypeStruct(dims, F32)


def ring(value, axes, step):
    count = 1
    for axis in axes:
        count *= lax.axis_size(axis)
    pairs = [(i, (i + step) % count) for i in range(count)]
    return lax.ppermute(value, axes if len(axes) > 1 else axes[0], pairs)


def along_dir(value, before, after):
    count = value.shape[0]
    low = ring(value[count - before :], ("dir",), 1)
    high = ring(value[:after], ("dir",), -1)
    return low, high


def along_next(value):
    low, high = along_dir(value, 12, 12)
    return jnp.concatenate([low, value, high], axis=0)


def along_patch(value, low_rows, high_rows):
    low = ring(value[:, low_rows[0] : low_rows[1]], PATCH, 1)
    high = ring(value[:, high_rows[0] : high_rows[1]], PATCH, -1)
    return low, high


def after(value, other):
    return lax.optimization_barrier((value, other))


def inside_lanes(first, count, per, total):
    plane = first + jnp.arange(count) // per
    return ((plane >= 0) & (plane < total)).astype(F32)


def on_device(right_side, guess, mask_fine, mask_next):
    position = lax.axis_index("dir")
    anywhere = pl.BlockSpec(memory_space=pl.ANY)
    vmem = pl.BlockSpec(memory_space=pltpu.VMEM)
    up, down = pl.pallas_call(
        pack_dir,
        out_shape=[shape_of(25, 24, 256), shape_of(23, 24, 256)],
        in_specs=[anywhere] * 2,
        out_specs=[vmem] * 2,
        scratch_shapes=[pltpu.SemaphoreType.DMA((4,))],
    )(guess, right_side)
    x_low = ring(up, ("dir",), 1)
    x_high = ring(down, ("dir",), -1)

    mask_fine, mask_next, up = lax.optimization_barrier((mask_fine, mask_next, up))
    fine = jnp.transpose(mask_fine, (1, 0, 2)).reshape(24, 48).astype(F32)
    following = mask_next[:, :, 0].T.astype(F32)
    plane = jnp.concatenate(
        [
            jnp.pad(fine, ((0, 0), (0, 80))),
            jnp.pad(following, ((0, 12), (0, 116))),
        ],
        axis=1,
    )
    m_low = ring(plane, ("dir",), 1)
    m_high = ring(plane, ("dir",), -1)
    fine = jnp.concatenate([m_low[:, 20:48], fine, m_high[:, :26]], axis=1)
    fine = fine * inside_lanes(24 * position - 14, 102, 2, 96)
    following = jnp.concatenate(
        [m_low[:12, 128:140], following, m_high[:12, 128:140]], axis=1
    )
    following = following * inside_lanes(12 * position - 12, 36, 1, 48)
    plane = jnp.concatenate(
        [
            jnp.pad(fine, ((0, 0), (0, 26))),
            jnp.pad(following, ((0, 12), (0, 92))),
        ],
        axis=1,
    )
    to_up, to_down = call(
        pack_patch,
        [shape_of(UP_ROWS, 128), shape_of(DOWN_ROWS, 128)],
        [],
        (guess, right_side, x_low, x_high, plane),
        10**6,
    )
    p_high = ring(to_down, PATCH, -1)
    p_low = ring(to_up, PATCH, 1)
    pieces = (guess, right_side, x_low, x_high, p_low, p_high, plane)

    window = ((2, 52, V0, LANES), F32)
    left0 = ((46, 48, 1024), BF16)
    w0 = ((1280, 256), BF16)
    columns = ((56, LANES), F32)
    x0, f1, mask1 = call(
        fine_pre,
        [shape_of(24, 24, 256), shape_of(12, 12, 128), shape_of(40, 128)],
        [window, window, window, left0, w0, ((28, 32, 128), F32), ((48, 128), F32), columns],
        pieces,
        10**10,
    )

    f1_own = along_next(f1)
    x0, f1_own = after(x0, f1_own)
    f1_low, f1_high = along_patch(f1_own, (0, 12), (0, 12))
    window1 = ((1, 36, 48, LANES), F32)
    left1 = ((30, 32, 512), BF16)
    w1 = ((640, 128), BF16)
    x1, f2 = call(
        next_pre,
        [shape_of(24, 24, 128), shape_of(64, 18, 128)],
        [window1, window1, window1, left1, w1, ((16, 16, 128), F32), ((48, 128), F32)],
        (f1_own, f1_low, f1_high, mask1),
        10**9,
    )

    x0_low, x0_high = along_dir(x0, 9, 9)
    x0_own = jnp.concatenate([x0_low, x0, x0_high], axis=0)
    x0_own, f2 = after(x0_own, f2)
    x0_low, x0_high = along_patch(x0_own, (8, 24), (0, 16))

    same = lax.all_to_all(f2, ("pz", "dir"), 0, 0)
    other = lax.ppermute(same, "core", [(0, 1), (1, 0)])
    (e2,) = call(
        coarse,
        [shape_of(17, 24, 128)],
        [
            ((1, 16, 144, LANES), F32),
            ((1, 16, 144, LANES), F32),
            ((12, 128, 512), BF16),
            w1,
            ((14, 112, 128), F32),
            ((112, 128), F32),
            ((1, 10, 64, LANES), F32),
            ((1, 10, 64, LANES), F32),
            w1,
            ((14, 24, 128), F32),
            ((2, 48, 128), F32),
        ],
        (same, other),
        4 * 10**9,
    )
    (y,) = call(
        next_post,
        [shape_of(12, 12, 128)],
        [window1, window1, window1, left1, w1, ((48, 128), F32), ((2, 48, 128), F32)],
        (f1_own, f1_low, f1_high, mask1, x1, e2),
        10**9,
    )
    y_low, y_high = along_dir(y, 9, 9)
    y_own = jnp.concatenate([y_low, y, y_high], axis=0)
    y_low, y_high = along_patch(y_own, (4, 12), (0, 9))
    (out,) = call(
        fine_post,
        [shape_of(24, 24, 256)],
        [
            window,
            window,
            window,
            left0,
            w0,
            ((48, 128), F32),
            ((2, 48, 128), F32),
            columns,
            window1,
            window1,
            window1,
            left1,
            w1,
        ],
        pieces
        + (x0_own, x0_low, x0_high, f1_own, f1_low, f1_high, mask1, y_own, y_low, y_high),
        10**10,
    )
    return out


def solution(mesh):
    pairs = Mesh(mesh.devices.reshape(16, 2, 4), ("pz", "core", "dir"))
    spec = P("dir", PATCH, None)
    return jax.shard_map(
        on_device, mesh=pairs, in_specs=(spec,) * 4, out_specs=spec, check_vma=False
    )
```

```python
import functools

import jax
import jax.numpy as jnp
from jax import lax
from jax.experimental import pallas as pl
from jax.experimental.pallas import tpu as pltpu
from jax.sharding import Mesh
from jax.sharding import PartitionSpec as P

F32 = jnp.float32
BF16 = jnp.bfloat16
LANES = 128

MASS = (2416.0, 1191.0, 120.0, 1.0)
STIFF = (80.0, -15.0, -24.0, -1.0)
ALPHA = 0.5 / (120.0 * 5040.0 * 5040.0)
PATCH = ("pz", "core")


def dot(a, b):
    return jnp.dot(a, b, preferred_element_type=F32)


def split(value):
    high = value.astype(BF16)
    return high, (value - high.astype(F32)).astype(BF16)


def dot_split(value, matrix):
    high, low = split(value)
    return dot(high, matrix) + dot(low, matrix)


def banded(rows, columns, size_r, size_c, coeffs, row_step, column_step, pairs=False):
    i = lax.broadcasted_iota(jnp.int32, (rows, columns), 0)
    j = lax.broadcasted_iota(jnp.int32, (rows, columns), 1)
    same = i >= 0
    if pairs:
        same = (i < 64) == (j < 64)
        i, j = jnp.where(i < 64, i, i - 64), jnp.where(j < 64, j, j - 64)
    at = row_step * i + column_step * j
    out = jnp.zeros((rows, columns), F32)
    for key, weight in coeffs.items():
        out = jnp.where(at == key, weight, out)
    return jnp.where((i < size_r) & (j < size_c) & same, out, 0.0).astype(BF16)


def fill_w(w_ref, depth, size, pairs=False):
    mass = {0: 2416.0, 1: 1192.0, -1: 1192.0, 2: 120.0, -2: 120.0, 3: 1.0, -3: 1.0}
    low = {1: -1.0, -1: -1.0}
    stiff = {0: 80.0, 1: -15.0, -1: -15.0, 2: -24.0, -2: -24.0, 3: -1.0, -3: -1.0}
    for block, table in enumerate((mass, mass, stiff, stiff, low)):
        w_ref[block * depth : (block + 1) * depth, :] = banded(
            depth, depth, size, size, table, 1, -1, pairs
        )


def restrict_w(rows, columns, size, pairs=False):
    taps = {-2: 0.125, -1: 0.5, 0: 0.75, 1: 0.5, 2: 0.125}
    return banded(rows, columns, size, size // 2, taps, 1, -2, pairs)


def prolong_w(rows, columns, size, pairs=False):
    taps = {-2: 0.125, -1: 0.5, 0: 0.75, 1: 0.5, 2: 0.125}
    return banded(rows, columns, size // 2, size, taps, -2, 1, pairs)


def stencil(x_ref, l_ref, u0, nu, v0, nv):
    tiles = x_ref.shape[0]
    depth = tiles * LANES

    def weigh(centre, one, two, three, taps):
        return taps[0] * centre + taps[1] * one + taps[2] * two + taps[3] * three

    for tile in range(tiles):
        for column in range(nv // 16):
            row = v0 + 16 * column

            def plane(u):
                x = [x_ref[tile, u, pl.ds(row - 3 + k, 16), :] for k in range(7)]
                one, two, three = x[2] + x[4], x[1] + x[5], x[0] + x[6]
                p = 2416.0 * x[3] + 1191.0 * one + 120.0 * two + three
                q = 80.0 * x[3] - 15.0 * one - 24.0 * two - three
                return p, q

            def emit(at, ps, qs):
                p1, p2, p3 = ps[2] + ps[4], ps[1] + ps[5], ps[0] + ps[6]
                q1, q2, q3 = qs[2] + qs[4], qs[1] + qs[5], qs[0] + qs[6]
                r = 2416.0 * ps[3] + 1191.0 * p1 + 120.0 * p2 + p3
                s = (80.0 * ps[3] - 15.0 * p1 - 24.0 * p2 - p3) + (
                    2416.0 * qs[3] + 1191.0 * q1 + 120.0 * q2 + q3
                )
                for part, value in enumerate(split(s) + split(r)):
                    lane = part * depth + tile * LANES
                    l_ref[at, 16 * column : 16 * column + 16, lane : lane + LANES] = value

            def several(first, count, carry):
                ps, qs = list(carry[:6]), list(carry[6:])
                for k in range(count):
                    p, q = plane(u0 + first + k + 3)
                    emit(first + k, ps + [p], qs + [q])
                    ps, qs = ps[1:] + [p], qs[1:] + [q]
                return tuple(ps + qs)

            start = [plane(u0 - 3 + k) for k in range(6)]
            carry = tuple([p for p, _ in start] + [q for _, q in start])
            groups = nu // 6
            if groups > 1:
                carry = lax.fori_loop(0, groups, lambda g, c: several(6 * g, 6, c), carry)
            elif groups == 1:
                carry = several(0, 6, carry)
            if nu % 6:
                several(6 * groups, nu % 6, carry)


def stencil_pairs(x_ref, l_ref, k0, nk, v0, nv):
    low = lax.broadcasted_iota(jnp.int32, (16, LANES), 1) < 64

    for column in range(nv // 16):
        row = v0 + 16 * column

        def plane(k):
            x = [x_ref[0, k, pl.ds(row - 3 + i, 16), :] for i in range(7)]
            one, two, three = x[2] + x[4], x[1] + x[5], x[0] + x[6]
            p = 2416.0 * x[3] + 1191.0 * one + 120.0 * two + three
            q = 80.0 * x[3] - 15.0 * one - 24.0 * two - three
            return p, pltpu.roll(p, 64, 1), q, pltpu.roll(q, 64, 1)

        def sums(own, other):
            one = other[2] + jnp.where(low, other[1], other[3])
            three = jnp.where(low, other[0], other[4]) + jnp.where(low, other[3], other[1])
            return own[2], one, own[1] + own[3], three

        def emit(at, planes):
            p, p1, p2, p3 = sums([t[0] for t in planes], [t[1] for t in planes])
            q, q1, q2, q3 = sums([t[2] for t in planes], [t[3] for t in planes])
            r = 2416.0 * p + 1191.0 * p1 + 120.0 * p2 + p3
            s = (80.0 * p - 15.0 * p1 - 24.0 * p2 - p3) + (
                2416.0 * q + 1191.0 * q1 + 120.0 * q2 + q3
            )
            for part, value in enumerate(split(s) + split(r)):
                l_ref[at, 16 * column : 16 * column + 16, part * LANES : (part + 1) * LANES] = value

        def several(first, count, carry):
            planes = [carry[4 * i : 4 * i + 4] for i in range(4)]
            for i in range(count):
                planes = planes + [plane(k0 + first + i + 2)]
                emit(first + i, planes)
                planes = planes[1:]
            return tuple(value for t in planes for value in t)

        carry = tuple(value for i in range(4) for value in plane(k0 - 2 + i))
        if nk > 6:
            lax.fori_loop(0, nk // 4, lambda g, c: several(4 * g, 4, c), carry)
        else:
            several(0, nk, carry)


def finish(l_ref, w_ref, nu, nv, use):
    depth = w_ref.shape[1]
    chunk = max(1, min(nu, 384 // nv))

    def some(first, count):
        left = l_ref[pl.ds(first, count), 0:nv, :].reshape(count * nv, 4 * depth)
        use(
            first,
            count,
            dot(left, w_ref[0 : 4 * depth, :])
            + dot(left[:, 0:depth], w_ref[4 * depth : 5 * depth, :]),
        )

    whole = nu // chunk
    if whole > 1:
        lax.fori_loop(0, whole, lambda c, _: some(c * chunk, chunk), None)
    elif whole == 1:
        some(0, chunk)
    if nu % chunk:
        some(whole * chunk, nu % chunk)


def sweep(x_ref, sf_ref, sa, l_ref, w_ref, u0, nu, v0, nv, apply=stencil):
    apply(x_ref, l_ref, u0, nu, v0, nv)

    def use(first, count, product):
        for tile in range(x_ref.shape[0]):
            at = (tile, pl.ds(u0 + first, count), pl.ds(v0, nv), slice(None))
            part = product[:, tile * LANES : (tile + 1) * LANES].reshape(count, nv, LANES)
            weight = sa if isinstance(sa, float) else sa[at]
            x_ref[at] = x_ref[at] + (sf_ref[at] - weight * part)

    finish(l_ref, w_ref, nu, nv, use)


def residual(x_ref, sf_ref, sa, l_ref, w_ref, rw, t_ref, scale, u0, nu, v0, nv, t0, apply=stencil):
    apply(x_ref, l_ref, u0, nu, v0, nv)

    def use(first, count, product):
        parts = []
        for tile in range(x_ref.shape[0]):
            at = (tile, pl.ds(u0 + first, count), pl.ds(v0, nv), slice(None))
            part = product[:, tile * LANES : (tile + 1) * LANES].reshape(count, nv, LANES)
            weight = sa if isinstance(sa, float) else sa[at]
            value = scale * (sf_ref[at] - weight * part)
            parts.append(value.reshape(count * nv, LANES))
        whole = parts[0] if len(parts) == 1 else jnp.concatenate(parts, axis=1)
        narrow = dot_split(whole, rw)
        t_ref[pl.ds(t0 + first, count), 0:nv, :] = narrow.reshape(count, nv, LANES)

    finish(l_ref, w_ref, nu, nv, use)


def narrow_plane(t_ref, tu_ref, j, nv, rows):
    at = [t_ref[2 * j + k, 0:nv, :] for k in range(5)]
    tu_ref[0:nv, :] = 0.125 * (at[0] + at[4]) + 0.5 * (at[1] + at[3]) + 0.75 * at[2]
    at = [tu_ref[pl.ds(k, rows, stride=2), :] for k in range(5)]
    return 0.125 * (at[0] + at[4]) + 0.5 * (at[1] + at[3]) + 0.75 * at[2]


def widen(read, even, tu_ref, z_ref, slot, rows):
    if even:
        plane = 0.125 * (read(-1) + read(1)) + 0.75 * read(0)
    else:
        plane = 0.5 * (read(0) + read(1))
    tu_ref[0 : plane.shape[0], :] = plane
    low, mid, high = (tu_ref[k : k + rows, :] for k in range(3))
    z_ref[slot, pl.ds(0, rows, stride=2), :] = 0.125 * (low + high) + 0.75 * mid
    z_ref[slot, pl.ds(1, rows, stride=2), :] = 0.5 * (mid + high)


def spread_mask(column, rows):
    return jnp.broadcast_to(column, (rows, LANES))


UB0, VB0, V0 = 14, 16, 64

UP_X, UP_F, DOWN_X, DOWN_F = 14, 11, 13, 10
OWN_UP, OWN_DOWN = 48 * (UP_X + UP_F), 48 * (DOWN_X + DOWN_F)
UP_MASK = 54 * UP_X + 42 * UP_F
DOWN_MASK = 54 * DOWN_X + 42 * DOWN_F
OUTER_UP, OUTER_DOWN = 1248, 1152


def put_plane(source, index, at, rows, target, top):
    for tile in range(2):
        lanes = slice(tile * LANES, (tile + 1) * LANES)
        first = 24 - rows if top else 0
        row = at + (2 * index + tile) * rows
        target[row : row + rows, :] = source[first : first + rows, lanes]


def pack_own(guess, load, plane, up, down, to_up, to_down):
    up[0:14] = guess[10:24]
    up[14:25] = load[13:24]
    up[25] = plane[...]
    down[0:13] = guess[0:13]
    down[13:23] = load[0:10]
    down[23] = plane[...]
    for u in range(24):
        put_plane(guess.at[u], u, 0, UP_X, to_up, True)
        put_plane(guess.at[u], u, 0, DOWN_X, to_down, False)
        put_plane(load.at[u], u, 48 * UP_X, UP_F, to_up, True)
        put_plane(load.at[u], u, 48 * DOWN_X, DOWN_F, to_down, False)


def pack_outer(low, high, plane, to_up, to_down):
    for u in range(27):
        source = low.at[u] if u < 14 else high.at[u - 14]
        put_plane(source, u, 0, UP_X, to_up, True)
        put_plane(source, u, 0, DOWN_X, to_down, False)
    for u in range(21):
        source = low.at[14 + u] if u < 11 else high.at[13 + u - 11]
        put_plane(source, u, 54 * UP_X, UP_F, to_up, True)
        put_plane(source, u, 54 * DOWN_X, DOWN_F, to_down, False)
    at = UP_MASK
    to_up[at : at + 14, :] = plane[10:24, 0:LANES]
    to_up[at + 14 : at + 26, :] = plane[0:12, LANES:]
    at = DOWN_MASK
    to_down[at : at + 13, :] = plane[0:13, 0:LANES]
    to_down[at + 13 : at + 25, :] = plane[0:12, LANES:]


def x_pieces(pieces, u, tile):
    guess, _, low, high, own_up, own_down, up, down, _ = pieces
    lanes = slice(tile * LANES, (tile + 1) * LANES)
    if 14 <= u < 38:
        centre, below, above, index = guess.at[u - 14], own_up, own_down, u - 14
    else:
        centre = low.at[u] if u < 14 else high.at[u - 38]
        below, above, index = up, down, u if u < 14 else u - 24
    row, line = (2 * index + tile) * UP_X, (2 * index + tile) * DOWN_X
    return below[row : row + UP_X, :], centre[:, lanes], above[line : line + DOWN_X, :]


def f_pieces(pieces, u, tile):
    _, load, low, high, own_up, own_down, up, down, _ = pieces
    lanes = slice(tile * LANES, (tile + 1) * LANES)
    if 11 <= u < 35:
        centre, below, above, index = load.at[u - 11], own_up, own_down, u - 11
        first, start = 48 * UP_X, 48 * DOWN_X
    else:
        centre = low.at[14 + u] if u < 11 else high.at[13 + u - 35]
        below, above, index = up, down, u if u < 11 else u - 24
        first, start = 54 * UP_X, 54 * DOWN_X
    row = first + (2 * index + tile) * UP_F
    line = start + (2 * index + tile) * DOWN_F
    return below[row : row + UP_F, :], centre[:, lanes], above[line : line + DOWN_F, :]


def fill_fine(pieces, m_ref, x_ref, sf_ref, sa_ref):
    up, down, plane = pieces[6:]
    m_ref[2:16, :] = up[UP_MASK : UP_MASK + 14, :]
    m_ref[16:40, :] = plane[:, 0:LANES]
    m_ref[40:53, :] = down[DOWN_MASK : DOWN_MASK + 13, :]
    for u in range(51):
        for tile in range(2):
            lane = slice(2 * u + tile, 2 * u + tile + 1)
            if x_ref is not None:
                ranges = ((2, 16), (16, 40), (40, 53))
                for (first, last), value in zip(ranges, x_pieces(pieces, u, tile)):
                    active = spread_mask(m_ref[first:last, lane], last - first)
                    x_ref[tile, u, first:last, :] = active * value
            if 3 <= u < 48:
                ranges = ((5, 16), (16, 40), (40, 50))
                for (first, last), value in zip(ranges, f_pieces(pieces, u - 3, tile)):
                    active = spread_mask(m_ref[first:last, lane], last - first)
                    sa_ref[tile, u, first:last, :] = ALPHA * active
                    sf_ref[tile, u, first:last, :] = (0.5 * active) * value


def fine_pre(
    guess, load, low, high, own_up, own_down, up, down, plane,
    x_out, f1_out, mask_out, x, sf, sa, l_ref, w_ref, t_ref, tu_ref, m_ref,
):
    fill_w(w_ref, 256, 256)
    pieces = (guess, load, low, high, own_up, own_down, up, down, plane)
    fill_fine(pieces, m_ref, x, sf, sa)
    mask_out[0:12, :] = up[UP_MASK + 14 : UP_MASK + 26, :]
    mask_out[12:24, :] = plane[0:12, LANES:]
    mask_out[24:36, :] = down[DOWN_MASK + 13 : DOWN_MASK + 25, :]
    mask_out[36:40, :] = jnp.zeros((4, LANES), F32)
    sweep(x, sf, sa, l_ref, w_ref, 3, 45, 5, 48)
    sweep(x, sf, sa, l_ref, w_ref, 6, 39, 8, 48)
    sweep(x, sf, sa, l_ref, w_ref, 9, 33, 11, 48)
    for tile in range(2):
        x_out[:, :, tile * LANES : (tile + 1) * LANES] = x[tile, 14:38, 16:40, :]
    rw = restrict_w(256, LANES, 256)
    residual(x, sf, sa, l_ref, w_ref, rw, t_ref, 2.0, 12, 27, 14, 32, 0)
    for j in range(12):
        f1_out[j] = narrow_plane(t_ref, tu_ref, j, 32, 12)


def fine_post(
    guess, load, low, high, own_up, own_down, up, down, plane,
    x_own, x_low, x_high, f1_own, f1_low, f1_high, mask1, y_own, y_low, y_high,
    out, x, sf, sa, l_ref, w_ref, tu_ref, z_ref, m_ref, y, sf1, sa1, l1_ref, w1_ref,
):
    fill_w(w_ref, 256, 256)
    fill_w(w1_ref, 128, 128)
    pieces = (guess, load, low, high, own_up, own_down, up, down, plane)
    fill_fine(pieces, m_ref, None, sf, sa)

    fill_next(f1_own, f1_low, f1_high, mask1, None, sf1, sa1)
    for u in range(30):
        for source, row, rows in ((y_low, 4, 8), (y_own, 12, 12), (y_high, 24, 9)):
            part = slice(row, row + rows)
            active = spread_mask(mask1[part, u + 3 : u + 4], rows)
            y[0, u + 3, part, :] = active * source[u]
    sweep(y, sf1, sa1, l1_ref, w1_ref, 7, 23, 7, 32)

    pw = prolong_w(LANES, 256, 256)
    for u in range(-9, 33):

        def read(k):
            return y[0, u // 2 + 12 + k, 6:30, :]

        widen(read, u % 2 == 0, tu_ref, z_ref, 0, 22)
        fine = dot_split(z_ref[0, 0:48, :], pw)
        for tile in range(2):
            lanes = slice(tile * LANES, (tile + 1) * LANES)
            x[tile, u + UB0, 6:50, :] = fine[0:44, lanes]
    for u in range(42):
        for tile in range(2):
            lanes = slice(tile * LANES, (tile + 1) * LANES)
            at = u + 5
            for source, row, rows, first in (
                (x_low, 7, 9, 7), (x_own, 16, 24, 0), (x_high, 40, 9, 0)
            ):
                part = slice(row, row + rows)
                active = spread_mask(m_ref[part, 2 * at + tile : 2 * at + tile + 1], rows)
                x[tile, at, part, :] = active * (
                    x[tile, at, part, :] + source[u, first : first + rows, lanes]
                )
    sweep(x, sf, sa, l_ref, w_ref, 8, 36, 10, 48)
    sweep(x, sf, sa, l_ref, w_ref, 11, 30, 13, 32)
    sweep(x, sf, sa, l_ref, w_ref, 14, 24, 16, 32)
    for tile in range(2):
        out[:, :, tile * LANES : (tile + 1) * LANES] = x[tile, 14:38, 16:40, :]


def fill_next(own, low, high, mask, x_ref, sf_ref, sa_ref):
    for u in range(36):
        for source, row in ((low, 0), (own, 12), (high, 24)):
            at = slice(row, row + 12)
            active = spread_mask(mask[at, u : u + 1], 12)
            value = (0.25 * active) * source[u]
            sa_ref[0, u, at, :] = ALPHA * active
            sf_ref[0, u, at, :] = value
            if x_ref is not None:
                x_ref[0, u, at, :] = value


def next_pre(own, low, high, mask, x_out, f2_out, x, sf, sa, l_ref, w_ref, t_ref, tu_ref):
    fill_w(w_ref, 128, 128)
    fill_next(own, low, high, mask, x, sf, sa)
    sweep(x, sf, sa, l_ref, w_ref, 3, 30, 3, 32)
    sweep(x, sf, sa, l_ref, w_ref, 6, 24, 6, 32)
    x_out[...] = x[0, 6:30, 6:30, :]
    rw = restrict_w(LANES, LANES, 128)
    residual(x, sf, sa, l_ref, w_ref, rw, t_ref, 4.0, 10, 15, 10, 16, 0)
    for j in range(3):
        even = narrow_plane(t_ref, tu_ref, 2 * j, 16, 6)
        odd = narrow_plane(t_ref, tu_ref, 2 * j + 1, 16, 6)
        tu_ref[24 + 6 * j : 30 + 6 * j, :] = even + pltpu.roll(odd, 64, 1)
    value = tu_ref[24:42, :]
    for peer in range(64):
        f2_out[peer] = value


def next_post(
    own, low, high, mask, x_own, e2,
    out, x, sf, sa, l_ref, w_ref, tu_ref, z_ref,
):
    fill_w(w_ref, 128, 128)
    fill_next(own, low, high, mask, None, sf, sa)
    pw = prolong_w(LANES, LANES, 128)
    for u in range(-6, 18):
        coarse = u // 2 + 5

        def read(k):
            return e2[coarse + k, 0:24, :]

        widen(read, u % 2 == 0, tu_ref, z_ref, 0, 16)
        x[0, u + 12, 4:36, :] = dot_split(z_ref[0, 0:32, :], pw)
    for u in range(6, 30):
        for row in (6, 18):
            at = slice(row, row + 12)
            active = spread_mask(mask[at, u : u + 1], 12)
            x[0, u, at, :] = active * (x[0, u, at, :] + x_own[u - 6, row - 6 : row + 6, :])
    sweep(x, sf, sa, l_ref, w_ref, 9, 18, 9, 32)
    sweep(x, sf, sa, l_ref, w_ref, 12, 12, 12, 16)
    out[...] = x[0, 12:24, 12:24, :]


def coarse(
    same, other, e_out, x, sf, l_ref, w_ref, t_ref, tu_ref, x3, sf3, w3_ref, b_ref, z_ref
):
    fill_w(w_ref, 128, 64, True)
    fill_w(w3_ref, 128, 32, True)
    pair, core = lax.axis_index("pz"), lax.axis_index("core")
    position = lax.axis_index("dir")

    for edge in (0, 1, 14, 15):
        x[0, edge] = jnp.zeros(x.shape[2:], F32)
    for edge in (0, 13):
        t_ref[edge] = jnp.zeros(t_ref.shape[1:], F32)

    def place(source, offset, row):
        index = lax.rem(pair + 16 + offset, 16)
        for d in range(4):
            for k in range(3):
                value = 0.125 * source[index * 4 + d, 6 * k : 6 * k + 6, :]
                x[0, 3 * d + k + 2, pl.ds(row, 6), :] = value
                sf[0, 3 * d + k + 2, pl.ds(row, 6), :] = value

    def even_patch(k, _):
        place(same, k - 5, 12 * k)

    def odd_patch(k, _):
        place(other, k - 5 + core, 12 * k + 6)

    lax.fori_loop(0, 11, even_patch, None)
    lax.fori_loop(0, 10, odd_patch, None)

    def smooth(u0, nu, values, loads, factors, v0, nv):
        sweep(values, loads, ALPHA, l_ref, factors, u0, nu, v0, nv, stencil_pairs)

    smooth(2, 12, x, sf, w_ref, 8, 112)
    smooth(2, 12, x, sf, w_ref, 11, 112)
    rw = restrict_w(LANES, LANES, 64, True)
    residual(
        x, sf, ALPHA, l_ref, w_ref, rw, t_ref, 8.0, 2, 12, 14, 112, 1, stencil_pairs
    )

    for edge in (0, 1, 8, 9):
        x3[0, edge] = jnp.zeros(x3.shape[2:], F32)

    def low_half(rows):
        return lax.broadcasted_iota(jnp.int32, (rows, LANES), 1) < 64

    def narrow(m, _):
        parts = []
        for odd in (0, 1):
            j = 2 * m + odd
            before, own, after = (t_ref[j + i, 0:112, :] for i in range(3))
            value = jnp.where(
                low_half(112), 0.125 * (before + after) + 0.75 * own, 0.5 * (before + own)
            )
            parts.append(value + pltpu.roll(value, 64, 1))
        tu_ref[0:112, :] = jnp.where(low_half(112), parts[0], parts[1])
        at = [tu_ref[pl.ds(i, 48, stride=2), :] for i in range(5)]
        value = 0.0625 * (0.125 * (at[0] + at[4]) + 0.5 * (at[1] + at[3]) + 0.75 * at[2])
        x3[0, m + 2, 4:52, :] = value
        sf3[0, m + 2, 4:52, :] = value

    lax.fori_loop(0, 6, narrow, None)
    smooth(2, 6, x3, sf3, w3_ref, 7, 48)
    smooth(2, 6, x3, sf3, w3_ref, 10, 48)
    smooth(2, 6, x3, sf3, w3_ref, 13, 32)
    smooth(2, 6, x3, sf3, w3_ref, 16, 32)
    smooth(2, 6, x3, sf3, w3_ref, 19, 32)

    pw = prolong_w(LANES, LANES, 64, True)
    for edge in (0, 13):
        b_ref[edge] = jnp.zeros(b_ref.shape[1:], F32)
    for m in range(6):
        value = x3[0, m + 2, 18:42, :]
        turned = pltpu.roll(value, 64, 1)
        b_ref[2 * m + 1] = jnp.where(low_half(24), value, turned)
        b_ref[2 * m + 2] = jnp.where(low_half(24), turned, value)

    def wide(k, _):
        before, own, after = (b_ref[k + i] for i in range(3))
        tu_ref[0:24, :] = jnp.where(
            low_half(24), 0.125 * (before + after) + 0.75 * own, 0.5 * (own + after)
        )
        first, mid, last = (tu_ref[i : i + 22, :] for i in range(3))
        z_ref[0, pl.ds(0, 22, stride=2), :] = 0.125 * (first + last) + 0.75 * mid
        z_ref[0, pl.ds(1, 22, stride=2), :] = 0.5 * (mid + last)
        fine = dot_split(z_ref[0, 0:48, :], pw)
        at = (0, k + 2, slice(46, 94), slice(None))
        x[at] = x[at] + fine

    lax.fori_loop(0, 12, wide, None)
    smooth(2, 12, x, sf, w_ref, 50, 32)
    smooth(2, 12, x, sf, w_ref, 53, 32)
    smooth(2, 12, x, sf, w_ref, 56, 16)

    for k in range(17):
        index = 3 * position + (k - 5) // 2
        inside = jnp.logical_and(index >= 0, index < 12)
        value = x[0, jnp.clip(index, 0, 11) + 2, 55:79, :]
        if k % 2 == 0:
            value = pltpu.roll(value, 64, 1)
        e_out[k] = jnp.where(inside & low_half(24), value, 0.0)


def call(body, outs, scratch, operands, flops):
    vmem = pl.BlockSpec(memory_space=pltpu.VMEM)
    size = 0
    for array in list(operands) + list(outs):
        dims = list(array.shape)
        dims[-1] = -(-dims[-1] // 128) * 128
        dims[-2] = -(-dims[-2] // 16) * 16
        count = 1
        for dim in dims:
            count *= dim
        size += 4 * count
    for shape, kind in scratch:
        count = 1
        for dim in shape:
            count *= dim
        size += count * (2 if kind == BF16 else 4)
    return pl.pallas_call(
        body,
        out_shape=list(outs),
        in_specs=[vmem] * len(operands),
        out_specs=[vmem] * len(outs),
        scratch_shapes=[pltpu.VMEM(shape, kind) for shape, kind in scratch],
        compiler_params=pltpu.CompilerParams(vmem_limit_bytes=size + (6 << 20)),
        cost_estimate=pl.CostEstimate(flops=flops, bytes_accessed=size, transcendentals=0),
    )(*operands)


def shape_of(*dims):
    return jax.ShapeDtypeStruct(dims, F32)


def ring(value, axes, step):
    count = 1
    for axis in axes:
        count *= lax.axis_size(axis)
    pairs = [(i, (i + step) % count) for i in range(count)]
    return lax.ppermute(value, axes if len(axes) > 1 else axes[0], pairs)


def along_dir(value, before, after):
    count = value.shape[0]
    low = ring(value[count - before :], ("dir",), 1)
    high = ring(value[:after], ("dir",), -1)
    return low, high


def along_next(value):
    low, high = along_dir(value, 12, 12)
    return jnp.concatenate([low, value, high], axis=0)


def along_patch(value, low_rows, high_rows):
    low = ring(value[:, low_rows[0] : low_rows[1]], PATCH, 1)
    high = ring(value[:, high_rows[0] : high_rows[1]], PATCH, -1)
    return low, high


def after(value, other):
    return lax.optimization_barrier((value, other))


def inside_lanes(first, count, per, total):
    plane = first + jnp.arange(count) // per
    return ((plane >= 0) & (plane < total)).astype(F32)


def on_device(right_side, guess, mask_fine, mask_next):
    position = lax.axis_index("dir")
    fine = jnp.transpose(mask_fine, (1, 0, 2)).reshape(24, 48).astype(F32)
    following = mask_next[:, :, 0].T.astype(F32)
    plane = jnp.concatenate(
        [
            jnp.pad(fine, ((0, 0), (0, 80))),
            jnp.pad(following, ((0, 12), (0, 116))),
        ],
        axis=1,
    )
    up, down, to_up, to_down = call(
        pack_own,
        [
            shape_of(26, 24, 256),
            shape_of(24, 24, 256),
            shape_of(OWN_UP, 128),
            shape_of(OWN_DOWN, 128),
        ],
        [],
        (guess, right_side, plane),
        10**6,
    )
    x_low = ring(up, ("dir",), 1)
    x_high = ring(down, ("dir",), -1)
    own_down = ring(to_down, PATCH, -1)
    own_up = ring(to_up, PATCH, 1)
    x_low, x_high, own_up, own_down = lax.optimization_barrier((x_low, x_high, own_up, own_down))
    m_low, m_high = x_low[25], x_high[23]
    fine = jnp.concatenate([m_low[:, 20:48], fine, m_high[:, :26]], axis=1)
    fine = fine * inside_lanes(24 * position - 14, 102, 2, 96)
    following = jnp.concatenate(
        [m_low[:12, 128:140], following, m_high[:12, 128:140]], axis=1
    )
    following = following * inside_lanes(12 * position - 12, 36, 1, 48)
    plane = jnp.concatenate(
        [
            jnp.pad(fine, ((0, 0), (0, 26))),
            jnp.pad(following, ((0, 12), (0, 92))),
        ],
        axis=1,
    )
    to_up, to_down = call(
        pack_outer,
        [shape_of(OUTER_UP, 128), shape_of(OUTER_DOWN, 128)],
        [],
        (x_low, x_high, plane),
        10**6,
    )
    p_high = ring(to_down, PATCH, -1)
    p_low = ring(to_up, PATCH, 1)
    pieces = (guess, right_side, x_low, x_high, own_up, own_down, p_low, p_high, plane)

    window = ((2, 52, V0, LANES), F32)
    w0 = ((1280, 256), BF16)
    w1 = ((640, 128), BF16)
    left0 = ((46, 48, 1024), BF16)
    columns = ((56, LANES), F32)
    x0, f1, mask1 = call(
        fine_pre,
        [shape_of(24, 24, 256), shape_of(12, 12, 128), shape_of(40, 128)],
        [window, window, window, left0, w0, ((28, 32, 128), F32), ((48, 128), F32), columns],
        pieces,
        10**10,
    )

    f1_own = along_next(f1)
    f1_low, f1_high = along_patch(f1_own, (0, 12), (0, 12))
    x0, f1_low = after(x0, f1_low)
    x0_low, x0_high = along_dir(x0, 9, 9)
    window1 = ((1, 36, 48, LANES), F32)
    left1 = ((30, 32, 512), BF16)
    x1, f2 = call(
        next_pre,
        [shape_of(24, 24, 128), shape_of(64, 18, 128)],
        [window1, window1, window1, left1, w1, ((16, 16, 128), F32), ((48, 128), F32)],
        (f1_own, f1_low, f1_high, mask1),
        10**9,
    )

    x0_own = jnp.concatenate([x0_low, x0, x0_high], axis=0)
    x0_own, f2 = after(x0_own, f2)
    x0_low, x0_high = along_patch(x0_own, (8, 24), (0, 16))
    same = lax.all_to_all(f2, ("pz", "dir"), 0, 0)
    other = lax.ppermute(same, "core", [(0, 1), (1, 0)])
    (e2,) = call(
        coarse,
        [shape_of(17, 24, 128)],
        [
            ((1, 16, 144, LANES), F32),
            ((1, 16, 144, LANES), F32),
            ((12, 128, 512), BF16),
            w1,
            ((14, 112, 128), F32),
            ((112, 128), F32),
            ((1, 10, 64, LANES), F32),
            ((1, 10, 64, LANES), F32),
            w1,
            ((14, 24, 128), F32),
            ((2, 48, 128), F32),
        ],
        (same, other),
        4 * 10**9,
    )
    (y,) = call(
        next_post,
        [shape_of(12, 12, 128)],
        [window1, window1, window1, left1, w1, ((48, 128), F32), ((2, 48, 128), F32)],
        (f1_own, f1_low, f1_high, mask1, x1, e2),
        10**9,
    )
    y_low, y_high = along_dir(y, 9, 9)
    y_own = jnp.concatenate([y_low, y, y_high], axis=0)
    y_low, y_high = along_patch(y_own, (4, 12), (0, 9))
    (out,) = call(
        fine_post,
        [shape_of(24, 24, 256)],
        [
            window,
            window,
            window,
            left0,
            w0,
            ((48, 128), F32),
            ((2, 48, 128), F32),
            columns,
            window1,
            window1,
            window1,
            left1,
            w1,
        ],
        pieces
        + (x0_own, x0_low, x0_high, f1_own, f1_low, f1_high, mask1, y_own, y_low, y_high),
        10**10,
    )
    return out


def solution(mesh):
    pairs = Mesh(mesh.devices.reshape(16, 2, 4), ("pz", "core", "dir"))
    spec = P("dir", PATCH, None)
    return jax.shard_map(
        on_device, mesh=pairs, in_specs=(spec,) * 4, out_specs=spec, check_vma=False
    )
```

```python
import functools

import jax
import jax.numpy as jnp
from jax import lax
from jax.experimental import pallas as pl
from jax.experimental.pallas import tpu as pltpu
from jax.sharding import Mesh
from jax.sharding import PartitionSpec as P

F32 = jnp.float32
BF16 = jnp.bfloat16
LANES = 128

MASS = (2416.0, 1191.0, 120.0, 1.0)
STIFF = (80.0, -15.0, -24.0, -1.0)
ALPHA = 0.5 / (120.0 * 5040.0 * 5040.0)
PATCH = ("pz", "core")


def dot(a, b):
    return jnp.dot(a, b, preferred_element_type=F32)


def split(value):
    high = value.astype(BF16)
    return high, (value - high.astype(F32)).astype(BF16)


def dot_split(value, matrix):
    high, low = split(value)
    return dot(high, matrix) + dot(low, matrix)


def banded(rows, columns, size_r, size_c, coeffs, row_step, column_step, pairs=False):
    i = lax.broadcasted_iota(jnp.int32, (rows, columns), 0)
    j = lax.broadcasted_iota(jnp.int32, (rows, columns), 1)
    same = i >= 0
    if pairs:
        same = (i < 64) == (j < 64)
        i, j = jnp.where(i < 64, i, i - 64), jnp.where(j < 64, j, j - 64)
    at = row_step * i + column_step * j
    out = jnp.zeros((rows, columns), F32)
    for key, weight in coeffs.items():
        out = jnp.where(at == key, weight, out)
    return jnp.where((i < size_r) & (j < size_c) & same, out, 0.0).astype(BF16)


def fill_w(w_ref, depth, size, pairs=False):
    i = lax.broadcasted_iota(jnp.int32, (depth, depth), 0)
    j = lax.broadcasted_iota(jnp.int32, (depth, depth), 1)
    inside = i >= 0
    if pairs:
        inside = (i < 64) == (j < 64)
        i, j = jnp.where(i < 64, i, i - 64), jnp.where(j < 64, j, j - 64)
    apart = jnp.where(inside & (i < size) & (j < size), jnp.abs(i - j), 9)

    def table(*taps):
        out = jnp.zeros((depth, depth), F32)
        for distance, weight in enumerate(taps):
            out = jnp.where(apart == distance, weight, out)
        return out.astype(BF16)

    mass = table(2416.0, 1192.0, 120.0, 1.0)
    stiff = table(80.0, -15.0, -24.0, -1.0)
    for block, matrix in enumerate((mass, mass, stiff, stiff, table(0.0, -1.0))):
        w_ref[block * depth : (block + 1) * depth, :] = matrix


def restrict_w(rows, columns, size, pairs=False):
    taps = {-2: 0.125, -1: 0.5, 0: 0.75, 1: 0.5, 2: 0.125}
    return banded(rows, columns, size, size // 2, taps, 1, -2, pairs)


def prolong_w(rows, columns, size, pairs=False):
    taps = {-2: 0.125, -1: 0.5, 0: 0.75, 1: 0.5, 2: 0.125}
    return banded(rows, columns, size // 2, size, taps, -2, 1, pairs)


def stencil(x_ref, l_ref, u0, nu, v0, nv):
    tiles = x_ref.shape[0]
    depth = tiles * LANES

    def weigh(centre, one, two, three, taps):
        return taps[0] * centre + taps[1] * one + taps[2] * two + taps[3] * three

    for tile in range(tiles):
        for column in range(nv // 16):
            row = v0 + 16 * column

            def plane(u):
                x = [x_ref[tile, u, pl.ds(row - 3 + k, 16), :] for k in range(7)]
                one, two, three = x[2] + x[4], x[1] + x[5], x[0] + x[6]
                p = 2416.0 * x[3] + 1191.0 * one + 120.0 * two + three
                q = 80.0 * x[3] - 15.0 * one - 24.0 * two - three
                return p, q

            def emit(at, ps, qs):
                p1, p2, p3 = ps[2] + ps[4], ps[1] + ps[5], ps[0] + ps[6]
                q1, q2, q3 = qs[2] + qs[4], qs[1] + qs[5], qs[0] + qs[6]
                r = 2416.0 * ps[3] + 1191.0 * p1 + 120.0 * p2 + p3
                s = (80.0 * ps[3] - 15.0 * p1 - 24.0 * p2 - p3) + (
                    2416.0 * qs[3] + 1191.0 * q1 + 120.0 * q2 + q3
                )
                for part, value in enumerate(split(s) + split(r)):
                    lane = part * depth + tile * LANES
                    l_ref[at, 16 * column : 16 * column + 16, lane : lane + LANES] = value

            def several(first, count, carry):
                ps, qs = list(carry[:6]), list(carry[6:])
                for k in range(count):
                    p, q = plane(u0 + first + k + 3)
                    emit(first + k, ps + [p], qs + [q])
                    ps, qs = ps[1:] + [p], qs[1:] + [q]
                return tuple(ps + qs)

            start = [plane(u0 - 3 + k) for k in range(6)]
            carry = tuple([p for p, _ in start] + [q for _, q in start])
            group = nu // 3 if nu >= 18 else nu
            groups = nu // group
            if groups > 1:
                carry = lax.fori_loop(0, groups, lambda g, c: several(group * g, group, c), carry)
            else:
                carry = several(0, group, carry)
            if nu % group:
                several(group * groups, nu % group, carry)


def stencil_pairs(x_ref, l_ref, k0, nk, v0, nv):
    low = lax.broadcasted_iota(jnp.int32, (16, LANES), 1) < 64

    for column in range(nv // 16):
        row = v0 + 16 * column

        def plane(k):
            x = [x_ref[0, k, pl.ds(row - 3 + i, 16), :] for i in range(7)]
            one, two, three = x[2] + x[4], x[1] + x[5], x[0] + x[6]
            p = 2416.0 * x[3] + 1191.0 * one + 120.0 * two + three
            q = 80.0 * x[3] - 15.0 * one - 24.0 * two - three
            return p, pltpu.roll(p, 64, 1), q, pltpu.roll(q, 64, 1)

        def sums(own, other):
            one = other[2] + jnp.where(low, other[1], other[3])
            three = jnp.where(low, other[0], other[4]) + jnp.where(low, other[3], other[1])
            return own[2], one, own[1] + own[3], three

        def emit(at, planes):
            p, p1, p2, p3 = sums([t[0] for t in planes], [t[1] for t in planes])
            q, q1, q2, q3 = sums([t[2] for t in planes], [t[3] for t in planes])
            r = 2416.0 * p + 1191.0 * p1 + 120.0 * p2 + p3
            s = (80.0 * p - 15.0 * p1 - 24.0 * p2 - p3) + (
                2416.0 * q + 1191.0 * q1 + 120.0 * q2 + q3
            )
            for part, value in enumerate(split(s) + split(r)):
                l_ref[at, 16 * column : 16 * column + 16, part * LANES : (part + 1) * LANES] = value

        def several(first, count, carry):
            planes = [carry[4 * i : 4 * i + 4] for i in range(4)]
            for i in range(count):
                planes = planes + [plane(k0 + first + i + 2)]
                emit(first + i, planes)
                planes = planes[1:]
            return tuple(value for t in planes for value in t)

        carry = tuple(value for i in range(4) for value in plane(k0 - 2 + i))
        if nk > 6:
            lax.fori_loop(0, nk // 4, lambda g, c: several(4 * g, 4, c), carry)
        else:
            several(0, nk, carry)


def finish(l_ref, w_ref, nu, nv, use):
    depth = w_ref.shape[1]
    chunk = max(1, min(nu, 1152 // nv))
    chunk = -(-nu // -(-nu // chunk))

    def some(first, count):
        left = l_ref[pl.ds(first, count), 0:nv, :].reshape(count * nv, 4 * depth)
        use(
            first,
            count,
            dot(left, w_ref[0 : 4 * depth, :])
            + dot(left[:, 0:depth], w_ref[4 * depth : 5 * depth, :]),
        )

    whole = nu // chunk
    if whole > 1:
        lax.fori_loop(0, whole, lambda c, _: some(c * chunk, chunk), None)
    elif whole == 1:
        some(0, chunk)
    if nu % chunk:
        some(whole * chunk, nu % chunk)


def sweep(x_ref, sf_ref, sa, l_ref, w_ref, u0, nu, v0, nv, apply=stencil):
    apply(x_ref, l_ref, u0, nu, v0, nv)

    def use(first, count, product):
        for tile in range(x_ref.shape[0]):
            at = (tile, pl.ds(u0 + first, count), pl.ds(v0, nv), slice(None))
            part = product[:, tile * LANES : (tile + 1) * LANES].reshape(count, nv, LANES)
            weight = sa if isinstance(sa, float) else sa[at]
            x_ref[at] = x_ref[at] + (sf_ref[at] - weight * part)

    finish(l_ref, w_ref, nu, nv, use)


def residual(x_ref, sf_ref, sa, l_ref, w_ref, rw, t_ref, scale, u0, nu, v0, nv, t0, apply=stencil):
    apply(x_ref, l_ref, u0, nu, v0, nv)

    def use(first, count, product):
        parts = []
        for tile in range(x_ref.shape[0]):
            at = (tile, pl.ds(u0 + first, count), pl.ds(v0, nv), slice(None))
            part = product[:, tile * LANES : (tile + 1) * LANES].reshape(count, nv, LANES)
            weight = sa if isinstance(sa, float) else sa[at]
            value = scale * (sf_ref[at] - weight * part)
            parts.append(value.reshape(count * nv, LANES))
        whole = parts[0] if len(parts) == 1 else jnp.concatenate(parts, axis=1)
        narrow = dot_split(whole, rw)
        t_ref[pl.ds(t0 + first, count), 0:nv, :] = narrow.reshape(count, nv, LANES)

    finish(l_ref, w_ref, nu, nv, use)


def narrow_plane(t_ref, tu_ref, j, nv, rows):
    at = [t_ref[2 * j + k, 0:nv, :] for k in range(5)]
    tu_ref[0:nv, :] = 0.125 * (at[0] + at[4]) + 0.5 * (at[1] + at[3]) + 0.75 * at[2]
    at = [tu_ref[pl.ds(k, rows, stride=2), :] for k in range(5)]
    return 0.125 * (at[0] + at[4]) + 0.5 * (at[1] + at[3]) + 0.75 * at[2]


def widen(read, even, tu_ref, z_ref, slot, rows):
    if even:
        plane = 0.125 * (read(-1) + read(1)) + 0.75 * read(0)
    else:
        plane = 0.5 * (read(0) + read(1))
    tu_ref[slot, 0 : plane.shape[0], :] = plane
    low, mid, high = (tu_ref[slot, k : k + rows, :] for k in range(3))
    z_ref[slot, pl.ds(0, rows, stride=2), :] = 0.125 * (low + high) + 0.75 * mid
    z_ref[slot, pl.ds(1, rows, stride=2), :] = 0.5 * (mid + high)


def spread_mask(column, rows):
    return jnp.broadcast_to(column, (rows, LANES))


UB0, VB0, V0 = 14, 16, 64

UP_X, UP_F, DOWN_X, DOWN_F = 14, 11, 13, 10
OWN_UP, OWN_DOWN = 48 * (UP_X + UP_F), 48 * (DOWN_X + DOWN_F)
UP_MASK = 54 * UP_X + 42 * UP_F
DOWN_MASK = 54 * DOWN_X + 42 * DOWN_F
OUTER_UP, OUTER_DOWN = 1248, 1152


def put_plane(source, index, at, rows, target, top):
    for tile in range(2):
        lanes = slice(tile * LANES, (tile + 1) * LANES)
        first = 24 - rows if top else 0
        row = at + (2 * index + tile) * rows
        target[row : row + rows, :] = source[first : first + rows, lanes]


def pack_own(guess, load, plane, up, down, to_up, to_down):
    up[0:14] = guess[10:24]
    up[14:25] = load[13:24]
    up[25] = plane[...]
    down[0:13] = guess[0:13]
    down[13:23] = load[0:10]
    down[23] = plane[...]
    for u in range(24):
        put_plane(guess.at[u], u, 0, UP_X, to_up, True)
        put_plane(guess.at[u], u, 0, DOWN_X, to_down, False)
        put_plane(load.at[u], u, 48 * UP_X, UP_F, to_up, True)
        put_plane(load.at[u], u, 48 * DOWN_X, DOWN_F, to_down, False)


def pack_outer(low, high, plane, to_up, to_down):
    for u in range(27):
        source = low.at[u] if u < 14 else high.at[u - 14]
        put_plane(source, u, 0, UP_X, to_up, True)
        put_plane(source, u, 0, DOWN_X, to_down, False)
    for u in range(21):
        source = low.at[14 + u] if u < 11 else high.at[13 + u - 11]
        put_plane(source, u, 54 * UP_X, UP_F, to_up, True)
        put_plane(source, u, 54 * DOWN_X, DOWN_F, to_down, False)
    at = UP_MASK
    to_up[at : at + 14, :] = plane[10:24, 0:LANES]
    to_up[at + 14 : at + 26, :] = plane[0:12, LANES:]
    at = DOWN_MASK
    to_down[at : at + 13, :] = plane[0:13, 0:LANES]
    to_down[at + 13 : at + 25, :] = plane[0:12, LANES:]


def x_pieces(pieces, u, tile):
    guess, _, low, high, own_up, own_down, up, down, _ = pieces
    lanes = slice(tile * LANES, (tile + 1) * LANES)
    if 14 <= u < 38:
        centre, below, above, index = guess.at[u - 14], own_up, own_down, u - 14
    else:
        centre = low.at[u] if u < 14 else high.at[u - 38]
        below, above, index = up, down, u if u < 14 else u - 24
    row, line = (2 * index + tile) * UP_X, (2 * index + tile) * DOWN_X
    return below[row : row + UP_X, :], centre[:, lanes], above[line : line + DOWN_X, :]


def f_pieces(pieces, u, tile):
    _, load, low, high, own_up, own_down, up, down, _ = pieces
    lanes = slice(tile * LANES, (tile + 1) * LANES)
    if 11 <= u < 35:
        centre, below, above, index = load.at[u - 11], own_up, own_down, u - 11
        first, start = 48 * UP_X, 48 * DOWN_X
    else:
        centre = low.at[14 + u] if u < 11 else high.at[13 + u - 35]
        below, above, index = up, down, u if u < 11 else u - 24
        first, start = 54 * UP_X, 54 * DOWN_X
    row = first + (2 * index + tile) * UP_F
    line = start + (2 * index + tile) * DOWN_F
    return below[row : row + UP_F, :], centre[:, lanes], above[line : line + DOWN_F, :]


def fill_fine(pieces, m_ref, x_ref, sf_ref, sa_ref):
    up, down, plane = pieces[6:]
    m_ref[2:16, :] = up[UP_MASK : UP_MASK + 14, :]
    m_ref[16:40, :] = plane[:, 0:LANES]
    m_ref[40:53, :] = down[DOWN_MASK : DOWN_MASK + 13, :]
    for u in range(51):
        for tile in range(2):
            lane = slice(2 * u + tile, 2 * u + tile + 1)
            if x_ref is not None:
                ranges = ((2, 16), (16, 40), (40, 53))
                for (first, last), value in zip(ranges, x_pieces(pieces, u, tile)):
                    active = spread_mask(m_ref[first:last, lane], last - first)
                    x_ref[tile, u, first:last, :] = active * value
            if 3 <= u < 48:
                ranges = ((5, 16), (16, 40), (40, 50))
                for (first, last), value in zip(ranges, f_pieces(pieces, u - 3, tile)):
                    active = spread_mask(m_ref[first:last, lane], last - first)
                    sa_ref[tile, u, first:last, :] = ALPHA * active
                    sf_ref[tile, u, first:last, :] = (0.5 * active) * value


def fine_pre(
    guess, load, low, high, own_up, own_down, up, down, plane,
    x_out, f1_out, mask_out, x, sf, sa, l_ref, w_ref, t_ref, tu_ref, m_ref,
):
    fill_w(w_ref, 256, 256)
    pieces = (guess, load, low, high, own_up, own_down, up, down, plane)
    fill_fine(pieces, m_ref, x, sf, sa)
    mask_out[0:12, :] = up[UP_MASK + 14 : UP_MASK + 26, :]
    mask_out[12:24, :] = plane[0:12, LANES:]
    mask_out[24:36, :] = down[DOWN_MASK + 13 : DOWN_MASK + 25, :]
    mask_out[36:40, :] = jnp.zeros((4, LANES), F32)
    sweep(x, sf, sa, l_ref, w_ref, 3, 45, 5, 48)
    sweep(x, sf, sa, l_ref, w_ref, 6, 39, 8, 48)
    sweep(x, sf, sa, l_ref, w_ref, 9, 33, 11, 48)
    for tile in range(2):
        x_out[:, :, tile * LANES : (tile + 1) * LANES] = x[tile, 14:38, 16:40, :]
    rw = restrict_w(256, LANES, 256)
    residual(x, sf, sa, l_ref, w_ref, rw, t_ref, 2.0, 12, 27, 14, 32, 0)
    for j in range(12):
        f1_out[j] = narrow_plane(t_ref, tu_ref, j, 32, 12)


def fine_post(
    guess, load, low, high, own_up, own_down, up, down, plane,
    x_own, x_low, x_high, f1_own, f1_low, f1_high, mask1, y_own, y_low, y_high,
    out, x, sf, sa, l_ref, w_ref, tu_ref, z_ref, m_ref, y, sf1, sa1, l1_ref, w1_ref,
):
    fill_w(w_ref, 256, 256)
    fill_w(w1_ref, 128, 128)
    pieces = (guess, load, low, high, own_up, own_down, up, down, plane)
    fill_fine(pieces, m_ref, None, sf, sa)

    fill_next(f1_own, f1_low, f1_high, mask1, None, sf1, sa1)
    for u in range(30):
        for source, row, rows in ((y_low, 4, 8), (y_own, 12, 12), (y_high, 24, 9)):
            part = slice(row, row + rows)
            active = spread_mask(mask1[part, u + 3 : u + 4], rows)
            y[0, u + 3, part, :] = active * source[u]
    sweep(y, sf1, sa1, l1_ref, w1_ref, 7, 23, 7, 32)

    pw = prolong_w(LANES, 256, 256)
    for u in range(-9, 33):

        def read(k):
            return y[0, u // 2 + 12 + k, 6:30, :]

        widen(read, u % 2 == 0, tu_ref, z_ref, u + 9, 22)
    for first in (0, 21):
        fine = dot_split(z_ref[first : first + 21].reshape(21 * 48, LANES), pw)
        for tile in range(2):
            lanes = slice(tile * LANES, (tile + 1) * LANES)
            x[tile, first + 5 : first + 26, 6:54, :] = fine[:, lanes].reshape(21, 48, LANES)
    for u in range(42):
        for tile in range(2):
            lanes = slice(tile * LANES, (tile + 1) * LANES)
            at = u + 5
            for source, row, rows, first in (
                (x_low, 7, 9, 7), (x_own, 16, 24, 0), (x_high, 40, 9, 0)
            ):
                part = slice(row, row + rows)
                active = spread_mask(m_ref[part, 2 * at + tile : 2 * at + tile + 1], rows)
                x[tile, at, part, :] = active * (
                    x[tile, at, part, :] + source[u, first : first + rows, lanes]
                )
    sweep(x, sf, sa, l_ref, w_ref, 8, 36, 10, 48)
    sweep(x, sf, sa, l_ref, w_ref, 11, 30, 13, 32)
    sweep(x, sf, sa, l_ref, w_ref, 14, 24, 16, 32)
    for tile in range(2):
        out[:, :, tile * LANES : (tile + 1) * LANES] = x[tile, 14:38, 16:40, :]


def fill_next(own, low, high, mask, x_ref, sf_ref, sa_ref):
    for u in range(36):
        for source, row in ((low, 0), (own, 12), (high, 24)):
            at = slice(row, row + 12)
            active = spread_mask(mask[at, u : u + 1], 12)
            value = (0.25 * active) * source[u]
            sa_ref[0, u, at, :] = ALPHA * active
            sf_ref[0, u, at, :] = value
            if x_ref is not None:
                x_ref[0, u, at, :] = value


def next_pre(own, low, high, mask, x_out, f2_out, x, sf, sa, l_ref, w_ref, t_ref, tu_ref):
    fill_w(w_ref, 128, 128)
    fill_next(own, low, high, mask, x, sf, sa)
    sweep(x, sf, sa, l_ref, w_ref, 3, 30, 3, 32)
    sweep(x, sf, sa, l_ref, w_ref, 6, 24, 6, 32)
    x_out[...] = x[0, 6:30, 6:30, :]
    rw = restrict_w(LANES, LANES, 128)
    residual(x, sf, sa, l_ref, w_ref, rw, t_ref, 4.0, 10, 15, 10, 16, 0)
    for j in range(3):
        even = narrow_plane(t_ref, tu_ref, 2 * j, 16, 6)
        odd = narrow_plane(t_ref, tu_ref, 2 * j + 1, 16, 6)
        tu_ref[24 + 6 * j : 30 + 6 * j, :] = even + pltpu.roll(odd, 64, 1)
    value = tu_ref[24:42, :]
    for peer in range(64):
        f2_out[peer] = value


def next_post(
    own, low, high, mask, x_own, e2,
    out, x, sf, sa, l_ref, w_ref, tu_ref, z_ref,
):
    fill_w(w_ref, 128, 128)
    fill_next(own, low, high, mask, None, sf, sa)
    pw = prolong_w(LANES, LANES, 128)
    for u in range(-6, 18):
        coarse = u // 2 + 5

        def read(k):
            return e2[coarse + k, 0:24, :]

        widen(read, u % 2 == 0, tu_ref, z_ref, u + 6, 16)
    fine = dot_split(z_ref[...].reshape(24 * 32, LANES), pw)
    x[0, 6:30, 4:36, :] = fine.reshape(24, 32, LANES)
    for u in range(6, 30):
        for row in (6, 18):
            at = slice(row, row + 12)
            active = spread_mask(mask[at, u : u + 1], 12)
            x[0, u, at, :] = active * (x[0, u, at, :] + x_own[u - 6, row - 6 : row + 6, :])
    sweep(x, sf, sa, l_ref, w_ref, 9, 18, 9, 32)
    sweep(x, sf, sa, l_ref, w_ref, 12, 12, 12, 16)
    out[...] = x[0, 12:24, 12:24, :]


def coarse(
    same, other, e_out, x, sf, l_ref, w_ref, t_ref, tu_ref, x3, sf3, w3_ref, b_ref, z_ref
):
    fill_w(w_ref, 128, 64, True)
    fill_w(w3_ref, 128, 32, True)
    pair, core = lax.axis_index("pz"), lax.axis_index("core")
    position = lax.axis_index("dir")

    for edge in (0, 1, 14, 15):
        x[0, edge] = jnp.zeros(x.shape[2:], F32)
    for edge in (0, 13):
        t_ref[edge] = jnp.zeros(t_ref.shape[1:], F32)

    def place(source, offset, row):
        index = lax.rem(pair + 16 + offset, 16)
        for d in range(4):
            for k in range(3):
                value = 0.125 * source[index * 4 + d, 6 * k : 6 * k + 6, :]
                x[0, 3 * d + k + 2, pl.ds(row, 6), :] = value
                sf[0, 3 * d + k + 2, pl.ds(row, 6), :] = value

    def even_patch(k, _):
        place(same, k - 5, 12 * k)

    def odd_patch(k, _):
        place(other, k - 5 + core, 12 * k + 6)

    lax.fori_loop(0, 11, even_patch, None)
    lax.fori_loop(0, 10, odd_patch, None)

    def smooth(u0, nu, values, loads, factors, v0, nv):
        sweep(values, loads, ALPHA, l_ref, factors, u0, nu, v0, nv, stencil_pairs)

    smooth(2, 12, x, sf, w_ref, 8, 112)
    smooth(2, 12, x, sf, w_ref, 11, 112)
    rw = restrict_w(LANES, LANES, 64, True)
    residual(
        x, sf, ALPHA, l_ref, w_ref, rw, t_ref, 8.0, 2, 12, 14, 112, 1, stencil_pairs
    )

    for edge in (0, 1, 8, 9):
        x3[0, edge] = jnp.zeros(x3.shape[2:], F32)

    def low_half(rows):
        return lax.broadcasted_iota(jnp.int32, (rows, LANES), 1) < 64

    def narrow(m, _):
        parts = []
        for odd in (0, 1):
            j = 2 * m + odd
            before, own, after = (t_ref[j + i, 0:112, :] for i in range(3))
            value = jnp.where(
                low_half(112), 0.125 * (before + after) + 0.75 * own, 0.5 * (before + own)
            )
            parts.append(value + pltpu.roll(value, 64, 1))
        tu_ref[0:112, :] = jnp.where(low_half(112), parts[0], parts[1])
        at = [tu_ref[pl.ds(i, 48, stride=2), :] for i in range(5)]
        value = 0.0625 * (0.125 * (at[0] + at[4]) + 0.5 * (at[1] + at[3]) + 0.75 * at[2])
        x3[0, m + 2, 4:52, :] = value
        sf3[0, m + 2, 4:52, :] = value

    lax.fori_loop(0, 6, narrow, None)
    smooth(2, 6, x3, sf3, w3_ref, 7, 48)
    smooth(2, 6, x3, sf3, w3_ref, 10, 48)
    smooth(2, 6, x3, sf3, w3_ref, 13, 32)
    smooth(2, 6, x3, sf3, w3_ref, 16, 32)
    smooth(2, 6, x3, sf3, w3_ref, 19, 32)

    pw = prolong_w(LANES, LANES, 64, True)
    for edge in (0, 13):
        b_ref[edge] = jnp.zeros(b_ref.shape[1:], F32)
    for m in range(6):
        value = x3[0, m + 2, 18:42, :]
        turned = pltpu.roll(value, 64, 1)
        b_ref[2 * m + 1] = jnp.where(low_half(24), value, turned)
        b_ref[2 * m + 2] = jnp.where(low_half(24), turned, value)

    def wide(k, _):
        before, own, after = (b_ref[k + i] for i in range(3))
        spread = tu_ref.at[pl.ds(24 * k, 24)]
        spread[...] = jnp.where(
            low_half(24), 0.125 * (before + after) + 0.75 * own, 0.5 * (own + after)
        )
        first, mid, last = (spread[i : i + 22, :] for i in range(3))
        z_ref[k, pl.ds(0, 22, stride=2), :] = 0.125 * (first + last) + 0.75 * mid
        z_ref[k, pl.ds(1, 22, stride=2), :] = 0.5 * (mid + last)

    for k in range(12):
        wide(k, None)
    fine = dot_split(z_ref[...].reshape(12 * 48, LANES), pw)
    at = (0, slice(2, 14), slice(46, 94), slice(None))
    x[at] = x[at] + fine.reshape(12, 48, LANES)
    smooth(2, 12, x, sf, w_ref, 50, 32)
    smooth(2, 12, x, sf, w_ref, 53, 32)
    smooth(2, 12, x, sf, w_ref, 56, 16)

    for k in range(17):
        index = 3 * position + (k - 5) // 2
        inside = jnp.logical_and(index >= 0, index < 12)
        value = x[0, jnp.clip(index, 0, 11) + 2, 55:79, :]
        if k % 2 == 0:
            value = pltpu.roll(value, 64, 1)
        e_out[k] = jnp.where(inside & low_half(24), value, 0.0)


def call(body, outs, scratch, operands, flops):
    vmem = pl.BlockSpec(memory_space=pltpu.VMEM)
    size = 0
    for array in list(operands) + list(outs):
        dims = list(array.shape)
        dims[-1] = -(-dims[-1] // 128) * 128
        dims[-2] = -(-dims[-2] // 16) * 16
        count = 1
        for dim in dims:
            count *= dim
        size += 4 * count
    for shape, kind in scratch:
        count = 1
        for dim in shape:
            count *= dim
        size += count * (2 if kind == BF16 else 4)
    return pl.pallas_call(
        body,
        out_shape=list(outs),
        in_specs=[vmem] * len(operands),
        out_specs=[vmem] * len(outs),
        scratch_shapes=[pltpu.VMEM(shape, kind) for shape, kind in scratch],
        compiler_params=pltpu.CompilerParams(vmem_limit_bytes=size + (6 << 20)),
        cost_estimate=pl.CostEstimate(flops=flops, bytes_accessed=size, transcendentals=0),
    )(*operands)


def shape_of(*dims):
    return jax.ShapeDtypeStruct(dims, F32)


def ring(value, axes, step):
    count = 1
    for axis in axes:
        count *= lax.axis_size(axis)
    pairs = [(i, (i + step) % count) for i in range(count)]
    return lax.ppermute(value, axes if len(axes) > 1 else axes[0], pairs)


def along_dir(value, before, after):
    count = value.shape[0]
    low = ring(value[count - before :], ("dir",), 1)
    high = ring(value[:after], ("dir",), -1)
    return low, high


def along_next(value):
    low, high = along_dir(value, 12, 12)
    return jnp.concatenate([low, value, high], axis=0)


def along_patch(value, low_rows, high_rows):
    low = ring(value[:, low_rows[0] : low_rows[1]], PATCH, 1)
    high = ring(value[:, high_rows[0] : high_rows[1]], PATCH, -1)
    return low, high


def after(value, other):
    return lax.optimization_barrier((value, other))


def inside_lanes(first, count, per, total):
    plane = first + jnp.arange(count) // per
    return ((plane >= 0) & (plane < total)).astype(F32)


def on_device(right_side, guess, mask_fine, mask_next):
    position = lax.axis_index("dir")
    fine = jnp.transpose(mask_fine, (1, 0, 2)).reshape(24, 48).astype(F32)
    following = mask_next[:, :, 0].T.astype(F32)
    plane = jnp.concatenate(
        [
            jnp.pad(fine, ((0, 0), (0, 80))),
            jnp.pad(following, ((0, 12), (0, 116))),
        ],
        axis=1,
    )
    up, down, to_up, to_down = call(
        pack_own,
        [
            shape_of(26, 24, 256),
            shape_of(24, 24, 256),
            shape_of(OWN_UP, 128),
            shape_of(OWN_DOWN, 128),
        ],
        [],
        (guess, right_side, plane),
        10**6,
    )
    x_low = ring(up, ("dir",), 1)
    x_high = ring(down, ("dir",), -1)
    own_down = ring(to_down, PATCH, -1)
    own_up = ring(to_up, PATCH, 1)
    x_low, x_high, own_up, own_down = lax.optimization_barrier((x_low, x_high, own_up, own_down))
    m_low, m_high = x_low[25], x_high[23]
    fine = jnp.concatenate([m_low[:, 20:48], fine, m_high[:, :26]], axis=1)
    fine = fine * inside_lanes(24 * position - 14, 102, 2, 96)
    following = jnp.concatenate(
        [m_low[:12, 128:140], following, m_high[:12, 128:140]], axis=1
    )
    following = following * inside_lanes(12 * position - 12, 36, 1, 48)
    plane = jnp.concatenate(
        [
            jnp.pad(fine, ((0, 0), (0, 26))),
            jnp.pad(following, ((0, 12), (0, 92))),
        ],
        axis=1,
    )
    to_up, to_down = call(
        pack_outer,
        [shape_of(OUTER_UP, 128), shape_of(OUTER_DOWN, 128)],
        [],
        (x_low, x_high, plane),
        10**6,
    )
    p_high = ring(to_down, PATCH, -1)
    p_low = ring(to_up, PATCH, 1)
    pieces = (guess, right_side, x_low, x_high, own_up, own_down, p_low, p_high, plane)

    window = ((2, 52, V0, LANES), F32)
    w0 = ((1280, 256), BF16)
    w1 = ((640, 128), BF16)
    left0 = ((46, 48, 1024), BF16)
    columns = ((56, LANES), F32)
    x0, f1, mask1 = call(
        fine_pre,
        [shape_of(24, 24, 256), shape_of(12, 12, 128), shape_of(40, 128)],
        [window, window, window, left0, w0, ((28, 32, 128), F32), ((48, 128), F32), columns],
        pieces,
        10**10,
    )

    f1_own = along_next(f1)
    f1_low, f1_high = along_patch(f1_own, (0, 12), (0, 12))
    x0, f1_low = after(x0, f1_low)
    x0_low, x0_high = along_dir(x0, 9, 9)
    window1 = ((1, 36, 48, LANES), F32)
    left1 = ((30, 32, 512), BF16)
    x1, f2 = call(
        next_pre,
        [shape_of(24, 24, 128), shape_of(64, 18, 128)],
        [window1, window1, window1, left1, w1, ((16, 16, 128), F32), ((48, 128), F32)],
        (f1_own, f1_low, f1_high, mask1),
        10**9,
    )

    x0_own = jnp.concatenate([x0_low, x0, x0_high], axis=0)
    x0_own, f2 = after(x0_own, f2)
    x0_low, x0_high = along_patch(x0_own, (8, 24), (0, 16))
    same = lax.all_to_all(f2, ("pz", "dir"), 0, 0)
    other = lax.ppermute(same, "core", [(0, 1), (1, 0)])
    (e2,) = call(
        coarse,
        [shape_of(17, 24, 128)],
        [
            ((1, 16, 144, LANES), F32),
            ((1, 16, 144, LANES), F32),
            ((12, 128, 512), BF16),
            w1,
            ((14, 112, 128), F32),
            ((288, 128), F32),
            ((1, 10, 64, LANES), F32),
            ((1, 10, 64, LANES), F32),
            w1,
            ((14, 24, 128), F32),
            ((12, 48, 128), F32),
        ],
        (same, other),
        4 * 10**9,
    )
    (y,) = call(
        next_post,
        [shape_of(12, 12, 128)],
        [window1, window1, window1, left1, w1, ((24, 24, 128), F32), ((24, 32, 128), F32)],
        (f1_own, f1_low, f1_high, mask1, x1, e2),
        10**9,
    )
    y_low, y_high = along_dir(y, 9, 9)
    y_own = jnp.concatenate([y_low, y, y_high], axis=0)
    y_low, y_high = along_patch(y_own, (4, 12), (0, 9))
    (out,) = call(
        fine_post,
        [shape_of(24, 24, 256)],
        [
            window,
            window,
            window,
            left0,
            w0,
            ((42, 24, 128), F32),
            ((42, 48, 128), F32),
            columns,
            window1,
            window1,
            window1,
            left1,
            w1,
        ],
        pieces
        + (x0_own, x0_low, x0_high, f1_own, f1_low, f1_high, mask1, y_own, y_low, y_high),
        10**10,
    )
    return out


def solution(mesh):
    pairs = Mesh(mesh.devices.reshape(16, 2, 4), ("pz", "core", "dir"))
    spec = P("dir", PATCH, None)
    return jax.shard_map(
        on_device, mesh=pairs, in_specs=(spec,) * 4, out_specs=spec, check_vma=False
    )
```

```python
import functools

import jax
import jax.numpy as jnp
from jax import lax
from jax.experimental import pallas as pl
from jax.experimental.pallas import tpu as pltpu
from jax.sharding import Mesh
from jax.sharding import PartitionSpec as P

F32 = jnp.float32
BF16 = jnp.bfloat16
LANES = 128

MASS = (2416.0, 1191.0, 120.0, 1.0)
STIFF = (80.0, -15.0, -24.0, -1.0)
ALPHA = 0.5 / (120.0 * 5040.0 * 5040.0)
PATCH = ("pz", "core")


def dot(a, b):
    return jnp.dot(a, b, preferred_element_type=F32)


def split(value):
    high = value.astype(BF16)
    return high, (value - high.astype(F32)).astype(BF16)


def dot_split(value, matrix):
    high, low = split(value)
    return dot(high, matrix) + dot(low, matrix)


def banded(rows, columns, size_r, size_c, coeffs, row_step, column_step, pairs=False):
    i = lax.broadcasted_iota(jnp.int32, (rows, columns), 0)
    j = lax.broadcasted_iota(jnp.int32, (rows, columns), 1)
    same = i >= 0
    if pairs:
        same = (i < 64) == (j < 64)
        i, j = jnp.where(i < 64, i, i - 64), jnp.where(j < 64, j, j - 64)
    at = row_step * i + column_step * j
    out = jnp.zeros((rows, columns), F32)
    for key, weight in coeffs.items():
        out = jnp.where(at == key, weight, out)
    return jnp.where((i < size_r) & (j < size_c) & same, out, 0.0).astype(BF16)


def fill_w(w_ref, depth, size, pairs=False):
    i = lax.broadcasted_iota(jnp.int32, (depth, depth), 0)
    j = lax.broadcasted_iota(jnp.int32, (depth, depth), 1)
    inside = i >= 0
    if pairs:
        inside = (i < 64) == (j < 64)
        i, j = jnp.where(i < 64, i, i - 64), jnp.where(j < 64, j, j - 64)
    apart = jnp.where(inside & (i < size) & (j < size), jnp.abs(i - j), 9)

    def table(*taps):
        out = jnp.zeros((depth, depth), F32)
        for distance, weight in enumerate(taps):
            out = jnp.where(apart == distance, weight, out)
        return out.astype(BF16)

    mass = table(2416.0, 1192.0, 120.0, 1.0)
    stiff = table(80.0, -15.0, -24.0, -1.0)
    for block, matrix in enumerate((mass, mass, stiff, stiff, table(0.0, -1.0))):
        w_ref[block * depth : (block + 1) * depth, :] = matrix


def restrict_w(rows, columns, size, pairs=False):
    taps = {-2: 0.125, -1: 0.5, 0: 0.75, 1: 0.5, 2: 0.125}
    return banded(rows, columns, size, size // 2, taps, 1, -2, pairs)


def prolong_w(rows, columns, size, pairs=False):
    taps = {-2: 0.125, -1: 0.5, 0: 0.75, 1: 0.5, 2: 0.125}
    return banded(rows, columns, size // 2, size, taps, -2, 1, pairs)


def stencil(x_ref, l_ref, u0, nu, v0, nv):
    tiles = x_ref.shape[0]
    depth = tiles * LANES

    def weigh(centre, one, two, three, taps):
        return taps[0] * centre + taps[1] * one + taps[2] * two + taps[3] * three

    for tile in range(tiles):
        for column in range(nv // 16):
            row = v0 + 16 * column

            def plane(u):
                x = [x_ref[tile, u, pl.ds(row - 3 + k, 16), :] for k in range(7)]
                one, two, three = x[2] + x[4], x[1] + x[5], x[0] + x[6]
                p = 2416.0 * x[3] + 1191.0 * one + 120.0 * two + three
                q = 80.0 * x[3] - 15.0 * one - 24.0 * two - three
                return p, q

            def emit(at, ps, qs):
                p1, p2, p3 = ps[2] + ps[4], ps[1] + ps[5], ps[0] + ps[6]
                q1, q2, q3 = qs[2] + qs[4], qs[1] + qs[5], qs[0] + qs[6]
                r = 2416.0 * ps[3] + 1191.0 * p1 + 120.0 * p2 + p3
                s = (80.0 * ps[3] - 15.0 * p1 - 24.0 * p2 - p3) + (
                    2416.0 * qs[3] + 1191.0 * q1 + 120.0 * q2 + q3
                )
                for part, value in enumerate(split(s) + split(r)):
                    lane = part * depth + tile * LANES
                    l_ref[at, 16 * column : 16 * column + 16, lane : lane + LANES] = value

            def several(first, count, carry):
                ps, qs = list(carry[:6]), list(carry[6:])
                for k in range(count):
                    p, q = plane(u0 + first + k + 3)
                    emit(first + k, ps + [p], qs + [q])
                    ps, qs = ps[1:] + [p], qs[1:] + [q]
                return tuple(ps + qs)

            start = [plane(u0 - 3 + k) for k in range(6)]
            carry = tuple([p for p, _ in start] + [q for _, q in start])
            several(0, nu, carry)


def stencil_pairs(x_ref, l_ref, k0, nk, v0, nv):
    low = lax.broadcasted_iota(jnp.int32, (16, LANES), 1) < 64

    for column in range(nv // 16):
        row = v0 + 16 * column

        def plane(k):
            x = [x_ref[0, k, pl.ds(row - 3 + i, 16), :] for i in range(7)]
            one, two, three = x[2] + x[4], x[1] + x[5], x[0] + x[6]
            p = 2416.0 * x[3] + 1191.0 * one + 120.0 * two + three
            q = 80.0 * x[3] - 15.0 * one - 24.0 * two - three
            return p, pltpu.roll(p, 64, 1), q, pltpu.roll(q, 64, 1)

        def sums(own, other):
            one = other[2] + jnp.where(low, other[1], other[3])
            three = jnp.where(low, other[0], other[4]) + jnp.where(low, other[3], other[1])
            return own[2], one, own[1] + own[3], three

        def emit(at, planes):
            p, p1, p2, p3 = sums([t[0] for t in planes], [t[1] for t in planes])
            q, q1, q2, q3 = sums([t[2] for t in planes], [t[3] for t in planes])
            r = 2416.0 * p + 1191.0 * p1 + 120.0 * p2 + p3
            s = (80.0 * p - 15.0 * p1 - 24.0 * p2 - p3) + (
                2416.0 * q + 1191.0 * q1 + 120.0 * q2 + q3
            )
            for part, value in enumerate(split(s) + split(r)):
                l_ref[at, 16 * column : 16 * column + 16, part * LANES : (part + 1) * LANES] = value

        def several(first, count, carry):
            planes = [carry[4 * i : 4 * i + 4] for i in range(4)]
            for i in range(count):
                planes = planes + [plane(k0 + first + i + 2)]
                emit(first + i, planes)
                planes = planes[1:]
            return tuple(value for t in planes for value in t)

        carry = tuple(value for i in range(4) for value in plane(k0 - 2 + i))
        several(0, nk, carry)


def finish(l_ref, w_ref, nu, nv, use):
    depth = w_ref.shape[1]
    chunk = max(1, min(nu, 1152 // nv))
    chunk = -(-nu // -(-nu // chunk))

    def some(first, count):
        left = l_ref[pl.ds(first, count), 0:nv, :].reshape(count * nv, 4 * depth)
        use(
            first,
            count,
            dot(left, w_ref[0 : 4 * depth, :])
            + dot(left[:, 0:depth], w_ref[4 * depth : 5 * depth, :]),
        )

    whole = nu // chunk
    if whole > 1:
        lax.fori_loop(0, whole, lambda c, _: some(c * chunk, chunk), None)
    elif whole == 1:
        some(0, chunk)
    if nu % chunk:
        some(whole * chunk, nu % chunk)


def sweep(x_ref, sf_ref, sa, l_ref, w_ref, u0, nu, v0, nv, apply=stencil):
    apply(x_ref, l_ref, u0, nu, v0, nv)

    def use(first, count, product):
        for tile in range(x_ref.shape[0]):
            at = (tile, pl.ds(u0 + first, count), pl.ds(v0, nv), slice(None))
            part = product[:, tile * LANES : (tile + 1) * LANES].reshape(count, nv, LANES)
            weight = sa if isinstance(sa, float) else sa[at]
            x_ref[at] = x_ref[at] + (sf_ref[at] - weight * part)

    finish(l_ref, w_ref, nu, nv, use)


def residual(x_ref, sf_ref, sa, l_ref, w_ref, rw, t_ref, scale, u0, nu, v0, nv, t0, apply=stencil):
    apply(x_ref, l_ref, u0, nu, v0, nv)

    def use(first, count, product):
        parts = []
        for tile in range(x_ref.shape[0]):
            at = (tile, pl.ds(u0 + first, count), pl.ds(v0, nv), slice(None))
            part = product[:, tile * LANES : (tile + 1) * LANES].reshape(count, nv, LANES)
            weight = sa if isinstance(sa, float) else sa[at]
            value = scale * (sf_ref[at] - weight * part)
            parts.append(value.reshape(count * nv, LANES))
        whole = parts[0] if len(parts) == 1 else jnp.concatenate(parts, axis=1)
        narrow = dot_split(whole, rw)
        t_ref[pl.ds(t0 + first, count), 0:nv, :] = narrow.reshape(count, nv, LANES)

    finish(l_ref, w_ref, nu, nv, use)


def narrow_plane(t_ref, tu_ref, j, nv, rows):
    at = [t_ref[2 * j + k, 0:nv, :] for k in range(5)]
    tu_ref[0:nv, :] = 0.125 * (at[0] + at[4]) + 0.5 * (at[1] + at[3]) + 0.75 * at[2]
    at = [tu_ref[pl.ds(k, rows, stride=2), :] for k in range(5)]
    return 0.125 * (at[0] + at[4]) + 0.5 * (at[1] + at[3]) + 0.75 * at[2]


def widen(read, even, tu_ref, z_ref, slot, rows):
    if even:
        plane = 0.125 * (read(-1) + read(1)) + 0.75 * read(0)
    else:
        plane = 0.5 * (read(0) + read(1))
    tu_ref[slot, 0 : plane.shape[0], :] = plane
    low, mid, high = (tu_ref[slot, k : k + rows, :] for k in range(3))
    z_ref[slot, pl.ds(0, rows, stride=2), :] = 0.125 * (low + high) + 0.75 * mid
    z_ref[slot, pl.ds(1, rows, stride=2), :] = 0.5 * (mid + high)


def spread_mask(column, rows):
    return jnp.broadcast_to(column, (rows, LANES))


UB0, VB0, V0 = 14, 16, 64

UP_X, UP_F, DOWN_X, DOWN_F = 14, 11, 13, 10
OWN_UP, OWN_DOWN = 48 * (UP_X + UP_F), 48 * (DOWN_X + DOWN_F)
UP_MASK = 54 * UP_X + 42 * UP_F
DOWN_MASK = 54 * DOWN_X + 42 * DOWN_F
OUTER_UP, OUTER_DOWN = 1248, 1152


def put_plane(source, index, at, rows, target, top):
    for tile in range(2):
        lanes = slice(tile * LANES, (tile + 1) * LANES)
        first = 24 - rows if top else 0
        row = at + (2 * index + tile) * rows
        target[row : row + rows, :] = source[first : first + rows, lanes]


def pack_own(guess, load, plane, up, down, to_up, to_down):
    up[0:14] = guess[10:24]
    up[14:25] = load[13:24]
    up[25] = plane[...]
    down[0:13] = guess[0:13]
    down[13:23] = load[0:10]
    down[23] = plane[...]
    for u in range(24):
        put_plane(guess.at[u], u, 0, UP_X, to_up, True)
        put_plane(guess.at[u], u, 0, DOWN_X, to_down, False)
        put_plane(load.at[u], u, 48 * UP_X, UP_F, to_up, True)
        put_plane(load.at[u], u, 48 * DOWN_X, DOWN_F, to_down, False)


def pack_outer(low, high, plane, to_up, to_down):
    for u in range(27):
        source = low.at[u] if u < 14 else high.at[u - 14]
        put_plane(source, u, 0, UP_X, to_up, True)
        put_plane(source, u, 0, DOWN_X, to_down, False)
    for u in range(21):
        source = low.at[14 + u] if u < 11 else high.at[13 + u - 11]
        put_plane(source, u, 54 * UP_X, UP_F, to_up, True)
        put_plane(source, u, 54 * DOWN_X, DOWN_F, to_down, False)
    at = UP_MASK
    to_up[at : at + 14, :] = plane[10:24, 0:LANES]
    to_up[at + 14 : at + 26, :] = plane[0:12, LANES:]
    at = DOWN_MASK
    to_down[at : at + 13, :] = plane[0:13, 0:LANES]
    to_down[at + 13 : at + 25, :] = plane[0:12, LANES:]


def x_pieces(pieces, u, tile):
    guess, _, low, high, own_up, own_down, up, down, _ = pieces
    lanes = slice(tile * LANES, (tile + 1) * LANES)
    if 14 <= u < 38:
        centre, below, above, index = guess.at[u - 14], own_up, own_down, u - 14
    else:
        centre = low.at[u] if u < 14 else high.at[u - 38]
        below, above, index = up, down, u if u < 14 else u - 24
    row, line = (2 * index + tile) * UP_X, (2 * index + tile) * DOWN_X
    return below[row : row + UP_X, :], centre[:, lanes], above[line : line + DOWN_X, :]


def f_pieces(pieces, u, tile):
    _, load, low, high, own_up, own_down, up, down, _ = pieces
    lanes = slice(tile * LANES, (tile + 1) * LANES)
    if 11 <= u < 35:
        centre, below, above, index = load.at[u - 11], own_up, own_down, u - 11
        first, start = 48 * UP_X, 48 * DOWN_X
    else:
        centre = low.at[14 + u] if u < 11 else high.at[13 + u - 35]
        below, above, index = up, down, u if u < 11 else u - 24
        first, start = 54 * UP_X, 54 * DOWN_X
    row = first + (2 * index + tile) * UP_F
    line = start + (2 * index + tile) * DOWN_F
    return below[row : row + UP_F, :], centre[:, lanes], above[line : line + DOWN_F, :]


def fill_fine(pieces, m_ref, x_ref, sf_ref, sa_ref):
    up, down, plane = pieces[6:]
    m_ref[2:16, :] = up[UP_MASK : UP_MASK + 14, :]
    m_ref[16:40, :] = plane[:, 0:LANES]
    m_ref[40:53, :] = down[DOWN_MASK : DOWN_MASK + 13, :]
    for u in range(51):
        for tile in range(2):
            lane = slice(2 * u + tile, 2 * u + tile + 1)
            if x_ref is not None:
                ranges = ((2, 16), (16, 40), (40, 53))
                for (first, last), value in zip(ranges, x_pieces(pieces, u, tile)):
                    active = spread_mask(m_ref[first:last, lane], last - first)
                    x_ref[tile, u, first:last, :] = active * value
            if 3 <= u < 48:
                ranges = ((5, 16), (16, 40), (40, 50))
                for (first, last), value in zip(ranges, f_pieces(pieces, u - 3, tile)):
                    active = spread_mask(m_ref[first:last, lane], last - first)
                    sa_ref[tile, u, first:last, :] = ALPHA * active
                    sf_ref[tile, u, first:last, :] = (0.5 * active) * value


def fine_pre(
    guess, load, low, high, own_up, own_down, up, down, plane,
    x_out, f1_out, mask_out, x, sf, sa, l_ref, w_ref, t_ref, tu_ref, m_ref,
):
    fill_w(w_ref, 256, 256)
    pieces = (guess, load, low, high, own_up, own_down, up, down, plane)
    fill_fine(pieces, m_ref, x, sf, sa)
    mask_out[0:12, :] = up[UP_MASK + 14 : UP_MASK + 26, :]
    mask_out[12:24, :] = plane[0:12, LANES:]
    mask_out[24:36, :] = down[DOWN_MASK + 13 : DOWN_MASK + 25, :]
    mask_out[36:40, :] = jnp.zeros((4, LANES), F32)
    sweep(x, sf, sa, l_ref, w_ref, 3, 45, 5, 48)
    sweep(x, sf, sa, l_ref, w_ref, 6, 39, 8, 48)
    sweep(x, sf, sa, l_ref, w_ref, 9, 33, 11, 48)
    for tile in range(2):
        x_out[:, :, tile * LANES : (tile + 1) * LANES] = x[tile, 14:38, 16:40, :]
    rw = restrict_w(256, LANES, 256)
    residual(x, sf, sa, l_ref, w_ref, rw, t_ref, 2.0, 12, 27, 14, 32, 0)
    for j in range(12):
        f1_out[j] = narrow_plane(t_ref, tu_ref, j, 32, 12)


def fine_post(
    guess, load, low, high, own_up, own_down, up, down, plane,
    x_own, x_low, x_high, f1_own, f1_low, f1_high, mask1, y_own, y_low, y_high,
    out, x, sf, sa, l_ref, w_ref, tu_ref, z_ref, m_ref, y, sf1, sa1, l1_ref, w1_ref,
):
    fill_w(w_ref, 256, 256)
    fill_w(w1_ref, 128, 128)
    pieces = (guess, load, low, high, own_up, own_down, up, down, plane)
    fill_fine(pieces, m_ref, None, sf, sa)

    fill_next(f1_own, f1_low, f1_high, mask1, None, sf1, sa1)
    for u in range(30):
        for source, row, rows in ((y_low, 4, 8), (y_own, 12, 12), (y_high, 24, 9)):
            part = slice(row, row + rows)
            active = spread_mask(mask1[part, u + 3 : u + 4], rows)
            y[0, u + 3, part, :] = active * source[u]
    sweep(y, sf1, sa1, l1_ref, w1_ref, 7, 23, 7, 32)

    pw = prolong_w(LANES, 256, 256)
    for u in range(-9, 33):

        def read(k):
            return y[0, u // 2 + 12 + k, 6:30, :]

        widen(read, u % 2 == 0, tu_ref, z_ref, u + 9, 22)
    for first in (0, 21):
        fine = dot_split(z_ref[first : first + 21].reshape(21 * 48, LANES), pw)
        for tile in range(2):
            lanes = slice(tile * LANES, (tile + 1) * LANES)
            x[tile, first + 5 : first + 26, 6:54, :] = fine[:, lanes].reshape(21, 48, LANES)
    for u in range(42):
        for tile in range(2):
            lanes = slice(tile * LANES, (tile + 1) * LANES)
            at = u + 5
            for source, row, rows, first in (
                (x_low, 7, 9, 7), (x_own, 16, 24, 0), (x_high, 40, 9, 0)
            ):
                part = slice(row, row + rows)
                active = spread_mask(m_ref[part, 2 * at + tile : 2 * at + tile + 1], rows)
                x[tile, at, part, :] = active * (
                    x[tile, at, part, :] + source[u, first : first + rows, lanes]
                )
    sweep(x, sf, sa, l_ref, w_ref, 8, 36, 10, 48)
    sweep(x, sf, sa, l_ref, w_ref, 11, 30, 13, 32)
    sweep(x, sf, sa, l_ref, w_ref, 14, 24, 16, 32)
    for tile in range(2):
        out[:, :, tile * LANES : (tile + 1) * LANES] = x[tile, 14:38, 16:40, :]


def fill_next(own, low, high, mask, x_ref, sf_ref, sa_ref):
    for u in range(36):
        for source, row in ((low, 0), (own, 12), (high, 24)):
            at = slice(row, row + 12)
            active = spread_mask(mask[at, u : u + 1], 12)
            value = (0.25 * active) * source[u]
            sa_ref[0, u, at, :] = ALPHA * active
            sf_ref[0, u, at, :] = value
            if x_ref is not None:
                x_ref[0, u, at, :] = value


def next_pre(own, low, high, mask, x_out, f2_out, x, sf, sa, l_ref, w_ref, t_ref, tu_ref):
    fill_w(w_ref, 128, 128)
    fill_next(own, low, high, mask, x, sf, sa)
    sweep(x, sf, sa, l_ref, w_ref, 3, 30, 3, 32)
    sweep(x, sf, sa, l_ref, w_ref, 6, 24, 6, 32)
    x_out[...] = x[0, 6:30, 6:30, :]
    rw = restrict_w(LANES, LANES, 128)
    residual(x, sf, sa, l_ref, w_ref, rw, t_ref, 4.0, 10, 15, 10, 16, 0)
    for j in range(3):
        even = narrow_plane(t_ref, tu_ref, 2 * j, 16, 6)
        odd = narrow_plane(t_ref, tu_ref, 2 * j + 1, 16, 6)
        tu_ref[24 + 6 * j : 30 + 6 * j, :] = even + pltpu.roll(odd, 64, 1)
    value = tu_ref[24:42, :]
    for peer in range(64):
        f2_out[peer] = value


def next_post(
    own, low, high, mask, x_own, e2,
    out, x, sf, sa, l_ref, w_ref, tu_ref, z_ref,
):
    fill_w(w_ref, 128, 128)
    fill_next(own, low, high, mask, None, sf, sa)
    pw = prolong_w(LANES, LANES, 128)
    for u in range(-6, 18):
        coarse = u // 2 + 5

        def read(k):
            return e2[coarse + k, 0:24, :]

        widen(read, u % 2 == 0, tu_ref, z_ref, u + 6, 16)
    fine = dot_split(z_ref[...].reshape(24 * 32, LANES), pw)
    x[0, 6:30, 4:36, :] = fine.reshape(24, 32, LANES)
    for u in range(6, 30):
        for row in (6, 18):
            at = slice(row, row + 12)
            active = spread_mask(mask[at, u : u + 1], 12)
            x[0, u, at, :] = active * (x[0, u, at, :] + x_own[u - 6, row - 6 : row + 6, :])
    sweep(x, sf, sa, l_ref, w_ref, 9, 18, 9, 32)
    sweep(x, sf, sa, l_ref, w_ref, 12, 12, 12, 16)
    out[...] = x[0, 12:24, 12:24, :]


def coarse(
    same, other, e_out, x, sf, l_ref, w_ref, t_ref, tu_ref, x3, sf3, w3_ref, b_ref, z_ref
):
    fill_w(w_ref, 128, 64, True)
    fill_w(w3_ref, 128, 32, True)
    pair, core = lax.axis_index("pz"), lax.axis_index("core")
    position = lax.axis_index("dir")

    for edge in (0, 1, 14, 15):
        x[0, edge] = jnp.zeros(x.shape[2:], F32)
    for edge in (0, 13):
        t_ref[edge] = jnp.zeros(t_ref.shape[1:], F32)

    def place(source, offset, row):
        index = lax.rem(pair + 16 + offset, 16)
        for d in range(4):
            for k in range(3):
                value = 0.125 * source[index * 4 + d, 6 * k : 6 * k + 6, :]
                x[0, 3 * d + k + 2, pl.ds(row, 6), :] = value
                sf[0, 3 * d + k + 2, pl.ds(row, 6), :] = value

    def even_patch(k, _):
        place(same, k - 5, 12 * k)

    def odd_patch(k, _):
        place(other, k - 5 + core, 12 * k + 6)

    lax.fori_loop(0, 11, even_patch, None)
    lax.fori_loop(0, 10, odd_patch, None)

    def smooth(u0, nu, values, loads, factors, v0, nv):
        sweep(values, loads, ALPHA, l_ref, factors, u0, nu, v0, nv, stencil_pairs)

    smooth(2, 12, x, sf, w_ref, 8, 112)
    smooth(2, 12, x, sf, w_ref, 11, 112)
    rw = restrict_w(LANES, LANES, 64, True)
    residual(
        x, sf, ALPHA, l_ref, w_ref, rw, t_ref, 8.0, 2, 12, 14, 112, 1, stencil_pairs
    )

    for edge in (0, 1, 8, 9):
        x3[0, edge] = jnp.zeros(x3.shape[2:], F32)

    def low_half(rows):
        return lax.broadcasted_iota(jnp.int32, (rows, LANES), 1) < 64

    def narrow(m, _):
        parts = []
        for odd in (0, 1):
            j = 2 * m + odd
            before, own, after = (t_ref[j + i, 0:112, :] for i in range(3))
            value = jnp.where(
                low_half(112), 0.125 * (before + after) + 0.75 * own, 0.5 * (before + own)
            )
            parts.append(value + pltpu.roll(value, 64, 1))
        tu_ref[0:112, :] = jnp.where(low_half(112), parts[0], parts[1])
        at = [tu_ref[pl.ds(i, 48, stride=2), :] for i in range(5)]
        value = 0.0625 * (0.125 * (at[0] + at[4]) + 0.5 * (at[1] + at[3]) + 0.75 * at[2])
        x3[0, m + 2, 4:52, :] = value
        sf3[0, m + 2, 4:52, :] = value

    lax.fori_loop(0, 6, narrow, None)
    smooth(2, 6, x3, sf3, w3_ref, 7, 48)
    smooth(2, 6, x3, sf3, w3_ref, 10, 48)
    smooth(2, 6, x3, sf3, w3_ref, 13, 32)
    smooth(2, 6, x3, sf3, w3_ref, 16, 32)
    smooth(2, 6, x3, sf3, w3_ref, 19, 32)

    pw = prolong_w(LANES, LANES, 64, True)
    for edge in (0, 13):
        b_ref[edge] = jnp.zeros(b_ref.shape[1:], F32)
    for m in range(6):
        value = x3[0, m + 2, 18:42, :]
        turned = pltpu.roll(value, 64, 1)
        b_ref[2 * m + 1] = jnp.where(low_half(24), value, turned)
        b_ref[2 * m + 2] = jnp.where(low_half(24), turned, value)

    def wide(k, _):
        before, own, after = (b_ref[k + i] for i in range(3))
        spread = tu_ref.at[pl.ds(24 * k, 24)]
        spread[...] = jnp.where(
            low_half(24), 0.125 * (before + after) + 0.75 * own, 0.5 * (own + after)
        )
        first, mid, last = (spread[i : i + 22, :] for i in range(3))
        z_ref[k, pl.ds(0, 22, stride=2), :] = 0.125 * (first + last) + 0.75 * mid
        z_ref[k, pl.ds(1, 22, stride=2), :] = 0.5 * (mid + last)

    for k in range(12):
        wide(k, None)
    fine = dot_split(z_ref[...].reshape(12 * 48, LANES), pw)
    at = (0, slice(2, 14), slice(46, 94), slice(None))
    x[at] = x[at] + fine.reshape(12, 48, LANES)
    smooth(2, 12, x, sf, w_ref, 50, 32)
    smooth(2, 12, x, sf, w_ref, 53, 32)
    smooth(2, 12, x, sf, w_ref, 56, 16)

    for k in range(17):
        index = 3 * position + (k - 5) // 2
        inside = jnp.logical_and(index >= 0, index < 12)
        value = x[0, jnp.clip(index, 0, 11) + 2, 55:79, :]
        if k % 2 == 0:
            value = pltpu.roll(value, 64, 1)
        e_out[k] = jnp.where(inside & low_half(24), value, 0.0)


def call(body, outs, scratch, operands, flops):
    vmem = pl.BlockSpec(memory_space=pltpu.VMEM)
    size = 0
    for array in list(operands) + list(outs):
        dims = list(array.shape)
        dims[-1] = -(-dims[-1] // 128) * 128
        dims[-2] = -(-dims[-2] // 16) * 16
        count = 1
        for dim in dims:
            count *= dim
        size += 4 * count
    for shape, kind in scratch:
        count = 1
        for dim in shape:
            count *= dim
        size += count * (2 if kind == BF16 else 4)
    return pl.pallas_call(
        body,
        out_shape=list(outs),
        in_specs=[vmem] * len(operands),
        out_specs=[vmem] * len(outs),
        scratch_shapes=[pltpu.VMEM(shape, kind) for shape, kind in scratch],
        compiler_params=pltpu.CompilerParams(vmem_limit_bytes=size + (6 << 20)),
        cost_estimate=pl.CostEstimate(flops=flops, bytes_accessed=size, transcendentals=0),
    )(*operands)


def shape_of(*dims):
    return jax.ShapeDtypeStruct(dims, F32)


def ring(value, axes, step):
    count = 1
    for axis in axes:
        count *= lax.axis_size(axis)
    pairs = [(i, (i + step) % count) for i in range(count)]
    return lax.ppermute(value, axes if len(axes) > 1 else axes[0], pairs)


def along_dir(value, before, after):
    count = value.shape[0]
    low = ring(value[count - before :], ("dir",), 1)
    high = ring(value[:after], ("dir",), -1)
    return low, high


def along_next(value):
    low, high = along_dir(value, 12, 12)
    return jnp.concatenate([low, value, high], axis=0)


def along_patch(value, low_rows, high_rows):
    low = ring(value[:, low_rows[0] : low_rows[1]], PATCH, 1)
    high = ring(value[:, high_rows[0] : high_rows[1]], PATCH, -1)
    return low, high


def after(value, other):
    return lax.optimization_barrier((value, other))


def inside_lanes(first, count, per, total):
    plane = first + jnp.arange(count) // per
    return ((plane >= 0) & (plane < total)).astype(F32)


def on_device(right_side, guess, mask_fine, mask_next):
    position = lax.axis_index("dir")
    fine = jnp.transpose(mask_fine, (1, 0, 2)).reshape(24, 48).astype(F32)
    following = mask_next[:, :, 0].T.astype(F32)
    plane = jnp.concatenate(
        [
            jnp.pad(fine, ((0, 0), (0, 80))),
            jnp.pad(following, ((0, 12), (0, 116))),
        ],
        axis=1,
    )
    up, down, to_up, to_down = call(
        pack_own,
        [
            shape_of(26, 24, 256),
            shape_of(24, 24, 256),
            shape_of(OWN_UP, 128),
            shape_of(OWN_DOWN, 128),
        ],
        [],
        (guess, right_side, plane),
        10**6,
    )
    x_low = ring(up, ("dir",), 1)
    x_high = ring(down, ("dir",), -1)
    own_down = ring(to_down, PATCH, -1)
    own_up = ring(to_up, PATCH, 1)
    x_low, x_high, own_up, own_down = lax.optimization_barrier((x_low, x_high, own_up, own_down))
    m_low, m_high = x_low[25], x_high[23]
    fine = jnp.concatenate([m_low[:, 20:48], fine, m_high[:, :26]], axis=1)
    fine = fine * inside_lanes(24 * position - 14, 102, 2, 96)
    following = jnp.concatenate(
        [m_low[:12, 128:140], following, m_high[:12, 128:140]], axis=1
    )
    following = following * inside_lanes(12 * position - 12, 36, 1, 48)
    plane = jnp.concatenate(
        [
            jnp.pad(fine, ((0, 0), (0, 26))),
            jnp.pad(following, ((0, 12), (0, 92))),
        ],
        axis=1,
    )
    to_up, to_down = call(
        pack_outer,
        [shape_of(OUTER_UP, 128), shape_of(OUTER_DOWN, 128)],
        [],
        (x_low, x_high, plane),
        10**6,
    )
    p_high = ring(to_down, PATCH, -1)
    p_low = ring(to_up, PATCH, 1)
    pieces = (guess, right_side, x_low, x_high, own_up, own_down, p_low, p_high, plane)

    window = ((2, 52, V0, LANES), F32)
    w0 = ((1280, 256), BF16)
    w1 = ((640, 128), BF16)
    left0 = ((46, 48, 1024), BF16)
    columns = ((56, LANES), F32)
    x0, f1, mask1 = call(
        fine_pre,
        [shape_of(24, 24, 256), shape_of(12, 12, 128), shape_of(40, 128)],
        [window, window, window, left0, w0, ((28, 32, 128), F32), ((48, 128), F32), columns],
        pieces,
        10**10,
    )

    f1_own = along_next(f1)
    f1_low, f1_high = along_patch(f1_own, (0, 12), (0, 12))
    x0, f1_low = after(x0, f1_low)
    x0_low, x0_high = along_dir(x0, 9, 9)
    window1 = ((1, 36, 48, LANES), F32)
    left1 = ((30, 32, 512), BF16)
    x1, f2 = call(
        next_pre,
        [shape_of(24, 24, 128), shape_of(64, 18, 128)],
        [window1, window1, window1, left1, w1, ((16, 16, 128), F32), ((48, 128), F32)],
        (f1_own, f1_low, f1_high, mask1),
        10**9,
    )

    x0_own = jnp.concatenate([x0_low, x0, x0_high], axis=0)
    x0_own, f2 = after(x0_own, f2)
    x0_low, x0_high = along_patch(x0_own, (8, 24), (0, 16))
    same = lax.all_to_all(f2, ("pz", "dir"), 0, 0)
    other = lax.ppermute(same, "core", [(0, 1), (1, 0)])
    (e2,) = call(
        coarse,
        [shape_of(17, 24, 128)],
        [
            ((1, 16, 144, LANES), F32),
            ((1, 16, 144, LANES), F32),
            ((12, 128, 512), BF16),
            w1,
            ((14, 112, 128), F32),
            ((288, 128), F32),
            ((1, 10, 64, LANES), F32),
            ((1, 10, 64, LANES), F32),
            w1,
            ((14, 24, 128), F32),
            ((12, 48, 128), F32),
        ],
        (same, other),
        4 * 10**9,
    )
    (y,) = call(
        next_post,
        [shape_of(12, 12, 128)],
        [window1, window1, window1, left1, w1, ((24, 24, 128), F32), ((24, 32, 128), F32)],
        (f1_own, f1_low, f1_high, mask1, x1, e2),
        10**9,
    )
    y_low, y_high = along_dir(y, 9, 9)
    y_own = jnp.concatenate([y_low, y, y_high], axis=0)
    y_low, y_high = along_patch(y_own, (4, 12), (0, 9))
    (out,) = call(
        fine_post,
        [shape_of(24, 24, 256)],
        [
            window,
            window,
            window,
            left0,
            w0,
            ((42, 24, 128), F32),
            ((42, 48, 128), F32),
            columns,
            window1,
            window1,
            window1,
            left1,
            w1,
        ],
        pieces
        + (x0_own, x0_low, x0_high, f1_own, f1_low, f1_high, mask1, y_own, y_low, y_high),
        10**10,
    )
    return out


def solution(mesh):
    pairs = Mesh(mesh.devices.reshape(16, 2, 4), ("pz", "core", "dir"))
    spec = P("dir", PATCH, None)
    return jax.shard_map(
        on_device, mesh=pairs, in_specs=(spec,) * 4, out_specs=spec, check_vma=False
    )
```
